512 devices in a mesh: row: 16 (over y, x), col: 32 (over z, core).
Axes of the slice: x: 4, y: 4, z: 16, core: 2. Of those that a mesh axis runs over, the one named last changes fastest.
Arguments:
- kernel: float32 [8192, 8192], P('row', 'col'), as said below
Outputs:
- factored: float32 [8192, 8192], P('row', 'col')
Inputs may be any that keep to these rules, and one draw needn't show every extreme that they name: In G's order the kernel is symmetric, and the diagonal blocks met by the 2 steps are positive definite and well conditioned.
All inputs are finite; a program needn't handle non-finite values.
Results may differ from the reference program's by a relative error of at most 0.0001.
Values sent between devices are 32-bit elements; how exact they have to be, the bound alone decides.
No kernel may reach another device: no remote copies, remote signals or barrier semaphores. Data moves between devices by JAX's collectives and lax.ppermute only.
A program may use at most 64 MiB of HBM per device.

```python
import math
import jax
import jax.numpy as jnp
from jax import lax

NB = 256
COLB = 1
PANELS = 2
ROWB = 2
M = 8192
N_ROW = 16
N_COL = 32


def draw_kernel(key, part):
    key = jax.random.fold_in(key, 7)
    first_key, second_key = jax.random.split(key, 2)
    noise = jax.random.uniform(first_key, (M, M), jnp.float32, -1.0, 1.0)
    mirrored = 0.5 * (noise + noise.T)
    diagonal = math.sqrt(NB) * (1.77 + 0.35 * jax.random.uniform(second_key, (M,), jnp.float32))
    places = jnp.arange(M, dtype=jnp.int32)
    matrix = jnp.where(places[:, None] == places[None, :], diagonal[:, None], mirrored)
    shaped = matrix.reshape(ROWB, N_ROW, NB, COLB, N_COL, NB)
    return shaped.transpose(1, 0, 2, 4, 3, 5).reshape(M, M).astype(jnp.float32)


def setup_inputs(seed: int = 0) -> dict:
    arg_keys = jax.random.split(jax.random.key(seed), 2)
    kernel = draw_kernel(jax.random.fold_in(arg_keys[1], 71), 0)
    return dict(kernel=kernel)


def to_global(stored):
    shaped = stored.reshape(N_ROW, ROWB, NB, N_COL, COLB, NB)
    return shaped.transpose(1, 0, 2, 4, 3, 5).reshape(M, M)

def to_stored(matrix):
    shaped = matrix.reshape(ROWB, N_ROW, NB, COLB, N_COL, NB)
    return shaped.transpose(1, 0, 2, 4, 3, 5).reshape(M, M)

def reference(kernel):
    highest = lax.Precision.HIGHEST
    matrix = to_global(kernel)
    for step in range(PANELS):
        start = step * NB
        finish = start + NB
        diag_factor = jnp.linalg.cholesky(matrix[start:finish, start:finish])
        identity = jnp.eye(NB, dtype=matrix.dtype)
        inverse = jax.scipy.linalg.solve_triangular(diag_factor, identity, lower=True)
        below = jnp.dot(matrix[finish:, start:finish], inverse.T, precision=highest)
        trailing = matrix[finish:, finish:] - jnp.dot(below, below.T, precision=highest)
        matrix = matrix.at[finish:, finish:].set(trailing)
        matrix = matrix.at[start:finish, start:].set(0.0)
        matrix = matrix.at[:start, start:finish].set(0.0)
        matrix = matrix.at[start:finish, start:finish].set(diag_factor)
        matrix = matrix.at[finish:, start:finish].set(below)
    return to_stored(matrix)
```

```python
import jax
import jax.numpy as jnp
from jax import lax
from jax.experimental import pallas as pl
from jax.experimental.pallas import tpu as pltpu
from jax.sharding import PartitionSpec as P

NB = 256
BASE = 32
LANES = 128
SUBS = 8
HIGHEST = lax.Precision.HIGHEST
VMEM_LIMIT = 24 * 1024 * 1024

CHIPS_Z = 16
PANEL_TREE = (
    ((0, 7),),
    ((0, 4), (7, 11)),
    ((0, 2), (4, 6), (7, 9), (11, 13)),
    ((0, 15), (2, 1), (4, 3), (6, 5), (7, 8), (9, 10), (11, 12), (13, 14)),
)
PIECE_TREE = (
    (((0, 8),), ((0, 4),), ((0, 12),)),
    (
        tuple((s, s + 2) for s in (0, 4, 8, 12)),
        tuple((s, (s + 15) % 16) for s in (0, 4, 8, 12)),
        tuple((s, s + 1) for s in (0, 4, 8, 12)),
    ),
)


def product(a, b, a_dim, b_dim):
    return lax.dot_general(
        a,
        b,
        (((a_dim,), (b_dim,)), ((), ())),
        precision=HIGHEST,
        preferred_element_type=jnp.float32,
    )


def small_inverse(rows, off):
    groups = BASE // SUBS
    lane = lax.broadcasted_iota(jnp.int32, (SUBS, LANES), 1)
    sub = lax.broadcasted_iota(jnp.int32, (SUBS, LANES), 0)
    cols = [[None] * groups for _ in range(BASE)]
    for c in range(BASE):
        for q in range(c // SUBS, groups):
            piece = rows[SUBS * q : SUBS * q + SUBS, off + c : off + c + 1]
            cols[c][q] = jnp.broadcast_to(piece, (SUBS, LANES))
    inv = [jnp.where(lane == sub + (off + SUBS * q), 1.0, 0.0) for q in range(groups)]
    scale = []
    for k in range(BASE):
        qk, rk = divmod(k, SUBS)
        root = lax.rsqrt(jnp.broadcast_to(cols[k][qk][rk : rk + 1], (SUBS, LANES)))
        recip = root * root
        for c in range(k + 1, BASE):
            qc, rc = divmod(c, SUBS)
            factor = jnp.broadcast_to(cols[k][qc][rc : rc + 1], (SUBS, LANES)) * recip
            for q in range(qc, groups):
                cols[c][q] = cols[c][q] - cols[k][q] * factor
        row = jnp.broadcast_to(inv[qk][rk : rk + 1], (SUBS, LANES)) * recip
        for q in range(qk, groups):
            update = cols[k][q] * row
            if q == qk:
                update = jnp.where(sub > rk, update, 0.0)
            inv[q] = inv[q] - update
        scale.append(root)
    out = []
    for q in range(groups):
        factor = scale[SUBS * q]
        for r in range(1, SUBS):
            factor = jnp.where(sub == r, scale[SUBS * q + r], factor)
        out.append(inv[q] * factor)
    return jnp.concatenate(out, axis=0)


def inverse_factor(square, out_ref, work):
    rows = lax.broadcasted_iota(jnp.int32, (NB, NB), 0)
    cols = lax.broadcasted_iota(jnp.int32, (NB, NB), 1)
    work[:, :NB] = square
    work[:, NB:] = jnp.where(rows == cols, 1.0, 0.0)
    for low in range(0, NB, BASE):
        tile = low // LANES * LANES
        off = low - tile
        high = low + BASE
        small = small_inverse(work[low:high, tile : tile + LANES], off)
        strip = product(small[:, off : off + BASE], work[low:high, :], 1, 0)
        out_ref[low:high, :] = strip[:, NB:]
        if high < NB:
            work[high:, :] = work[high:, :] - product(strip[:, high:NB], strip, 0, 0)


def first_kernel(square_ref, inv_ref, work):
    inverse_factor(square_ref[...], inv_ref, work)


def second_kernel(inv0_ref, upper_ref, square_ref, turned_ref, inv_ref, work):
    turned = product(inv0_ref[...], upper_ref[...], 1, 0)
    turned_ref[...] = turned
    inverse_factor(square_ref[...] - product(turned, turned, 0, 0), inv_ref, work)


def final_kernel(mine_ref, own_ref, other_ref, cols_ref, inv0_ref, turned_ref, inv1_ref, out_ref):
    row = lax.axis_index("row")
    col = lax.axis_index("col")
    core0 = lax.rem(col, 2) == 0
    rows_in = lax.broadcasted_iota(jnp.int32, (NB, NB), 0)
    cols_in = lax.broadcasted_iota(jnp.int32, (NB, NB), 1)
    inv0 = inv0_ref[...]
    turned = turned_ref[...]
    inv1 = inv1_ref[...]
    right0 = product(inv0, cols_ref[0], 1, 0)
    right1 = product(inv1, cols_ref[1] - product(turned, right0, 0, 0), 1, 0)
    for block in range(2):
        place = pl.ds(block * NB, NB)
        label = row + 16 * block
        own = own_ref[place, :]
        other = other_ref[place, :]
        panel0 = jnp.where(core0, own, other)
        panel1 = jnp.where(core0, other, own)
        left0 = product(panel0, inv0, 1, 1)
        left1 = product(panel1 - product(left0, turned, 1, 0), inv1, 1, 1)

        @pl.when(col >= 2)
        def _():
            trailing = mine_ref[place, :] - product(left0, right0, 1, 0) - product(left1, right1, 1, 0)
            out_ref[place, :] = jnp.where(label >= 2, trailing, 0.0)

        @pl.when(col < 2)
        def _():
            panel = jnp.where(col == 0, left0, left1)
            keep = (label > col) | ((label == col) & (rows_in >= cols_in))
            out_ref[place, :] = jnp.where(keep, panel, 0.0)


def call(body, outs, scratch):
    return pl.pallas_call(
        body,
        out_shape=outs,
        scratch_shapes=scratch,
        compiler_params=pltpu.CompilerParams(vmem_limit_bytes=VMEM_LIMIT),
    )


def both_cores(pairs, mirror):
    out = []
    for s, t in pairs:
        out.append((2 * s, 2 * t))
        if mirror:
            s, t = (CHIPS_Z - s) % CHIPS_Z, (CHIPS_Z - t) % CHIPS_Z
        out.append((2 * s + 1, 2 * t + 1))
    return out


def swap_cores(value):
    return lax.ppermute(value, "col", [(c, c ^ 1) for c in range(2 * CHIPS_Z)])


def local(kernel):
    square = jax.ShapeDtypeStruct((NB, NB), jnp.float32)
    work = [pltpu.VMEM((NB, 2 * NB), jnp.float32)]
    col = lax.axis_index("col")
    bottom = col < 2
    core0 = col % 2 == 0

    panel = jnp.where(bottom, kernel, 0.0)
    scattered = lax.all_to_all(kernel[:NB].reshape(16, 16, NB), "row", 0, 0)
    pieces = scattered[:2]
    swapped = swap_cores(pieces)
    lead = jnp.stack(
        [
            jnp.where(core0, pieces[0], swapped[0]),
            jnp.where(core0, swapped[0], pieces[0]),
            jnp.where(core0, swapped[1], pieces[1]),
        ]
    )
    lead = jnp.where(bottom, lead, 0.0)
    for stage in PIECE_TREE:
        lead = lead + sum(lax.ppermute(lead, "col", both_cores(p, False)) for p in stage)
    mine = jnp.concatenate([pieces, lead])
    gathered = lax.all_to_all(jnp.broadcast_to(mine[None], (16,) + mine.shape), "row", 0, 0)
    gathered = gathered.transpose(1, 0, 2, 3).reshape(5, NB, NB)

    for pairs in PANEL_TREE:
        panel = panel + lax.ppermute(panel, "col", both_cores(pairs, True))
    other = swap_cores(panel)

    inv0 = call(first_kernel, square, work)(gathered[2])
    turned, inv1 = call(second_kernel, (square, square), work)(inv0, gathered[3], gathered[4])
    return call(final_kernel, jax.ShapeDtypeStruct(kernel.shape, jnp.float32), [])(
        kernel, panel, other, gathered[:2], inv0, turned, inv1
    )


def solution(mesh):
    return jax.shard_map(
        local, mesh=mesh, in_specs=(P("row", "col"),), out_specs=P("row", "col"), check_vma=False
    )
```

```python
import jax
import jax.numpy as jnp
from jax import lax
from jax.experimental import pallas as pl
from jax.experimental.pallas import tpu as pltpu
from jax.sharding import PartitionSpec as P

NB = 256
BASE = 32
LANES = 128
SUBS = 8
HIGHEST = lax.Precision.HIGHEST
VMEM_LIMIT = 10 * 1024 * 1024

CHIPS_Z = 16
PANEL_TREE = (
    ((0, 7),),
    ((0, 4), (7, 11)),
    ((0, 2), (4, 6), (7, 9), (11, 13)),
    ((0, 15), (2, 1), (4, 3), (6, 5), (7, 8), (9, 10), (11, 12), (13, 14)),
)
PIECE_TREE = (
    (((0, 12),), ((0, 4),), ((0, 8),)),
    (
        tuple((s, s + 1) for s in (0, 4, 8, 12)),
        tuple((s, (s + 15) % 16) for s in (0, 4, 8, 12)),
        tuple((s, s + 2) for s in (0, 4, 8, 12)),
    ),
)


def product(a, b, a_dim, b_dim):
    return lax.dot_general(
        a,
        b,
        (((a_dim,), (b_dim,)), ((), ())),
        precision=HIGHEST,
        preferred_element_type=jnp.float32,
    )


def small_inverse(rows, off):
    groups = BASE // SUBS
    lane = lax.broadcasted_iota(jnp.int32, (SUBS, LANES), 1)
    sub = lax.broadcasted_iota(jnp.int32, (SUBS, LANES), 0)
    cols = [[None] * groups for _ in range(BASE)]
    for c in range(BASE):
        for q in range(c // SUBS, groups):
            piece = rows[SUBS * q : SUBS * q + SUBS, off + c : off + c + 1]
            cols[c][q] = jnp.broadcast_to(piece, (SUBS, LANES))
    inv = [jnp.where(lane == sub + (off + SUBS * q), 1.0, 0.0) for q in range(groups)]
    scale = []
    for k in range(BASE):
        qk, rk = divmod(k, SUBS)
        root = lax.rsqrt(jnp.broadcast_to(cols[k][qk][rk : rk + 1], (SUBS, LANES)))
        recip = root * root
        for c in range(k + 1, BASE):
            qc, rc = divmod(c, SUBS)
            factor = jnp.broadcast_to(cols[k][qc][rc : rc + 1], (SUBS, LANES)) * recip
            for q in range(qc, groups):
                cols[c][q] = cols[c][q] - cols[k][q] * factor
        row = jnp.broadcast_to(inv[qk][rk : rk + 1], (SUBS, LANES)) * recip
        for q in range(qk, groups):
            update = cols[k][q] * row
            if q == qk:
                update = jnp.where(sub > rk, update, 0.0)
            inv[q] = inv[q] - update
        scale.append(root)
    out = []
    for q in range(groups):
        factor = scale[SUBS * q]
        for r in range(1, SUBS):
            factor = jnp.where(sub == r, scale[SUBS * q + r], factor)
        out.append(inv[q] * factor)
    return jnp.concatenate(out, axis=0)


def inverse_factor(square, out_ref, work):
    rows = lax.broadcasted_iota(jnp.int32, (NB, NB), 0)
    cols = lax.broadcasted_iota(jnp.int32, (NB, NB), 1)
    work[:, :NB] = square
    work[:, NB:] = jnp.where(rows == cols, 1.0, 0.0)
    for low in range(0, NB, BASE):
        tile = low // LANES * LANES
        off = low - tile
        high = low + BASE
        small = small_inverse(work[low:high, tile : tile + LANES], off)
        strip = product(small[:, off : off + BASE], work[low:high, :], 1, 0)
        out_ref[low:high, :] = strip[:, NB:]
        if high < NB:
            work[high:, :] = work[high:, :] - product(strip[:, high:NB], strip, 0, 0)


def first_kernel(lead_ref, inv_ref, work):
    inverse_factor(lead_ref[:, 0].reshape(NB, NB), inv_ref, work)


def second_kernel(inv0_ref, lead_ref, turned_ref, inv_ref, work):
    turned = product(inv0_ref[...], lead_ref[:, 1].reshape(NB, NB), 1, 0)
    turned_ref[...] = turned
    square = lead_ref[:, 2].reshape(NB, NB) - product(turned, turned, 0, 0)
    inverse_factor(square, inv_ref, work)


def lead_kernel(first_ref, swapped_ref, lead_ref):
    col = lax.axis_index("col")
    bottom = col < 2
    core0 = lax.rem(col, 2) == 0
    first = jnp.where(bottom, first_ref[...], 0.0)
    swapped = jnp.where(bottom, swapped_ref[...], 0.0)
    lead_ref[0] = jnp.where(core0, first[0], swapped[0])
    lead_ref[1] = jnp.where(core0, swapped[0], first[0])
    lead_ref[2] = jnp.where(core0, swapped[1], first[1])


def mask_kernel(value_ref, out_ref):
    out_ref[...] = jnp.where(lax.axis_index("col") < 2, value_ref[...], 0.0)


def sum_kernel(*refs):
    total = refs[0][...]
    for ref in refs[1:-1]:
        total = total + ref[...]
    refs[-1][...] = total


def spread_kernel(early_ref, late_ref, base_ref, a_ref, b_ref, c_ref, out_ref):
    total = base_ref[...] + a_ref[...] + b_ref[...] + c_ref[...]
    pieces = early_ref[...] + late_ref[...]
    for target in range(out_ref.shape[0]):
        out_ref[target, :3] = total
        out_ref[target, 3:] = pieces


def factors_kernel(cols_ref, inv0_ref, turned_ref, inv1_ref, x0_ref, x1_ref):
    col = lax.axis_index("col")
    inv0 = inv0_ref[...]
    turned = turned_ref[...]
    inv1 = inv1_ref[...]

    @pl.when(col >= 2)
    def _():
        right0 = product(inv0, cols_ref[:, 3].reshape(NB, NB), 1, 0)
        below = cols_ref[:, 4].reshape(NB, NB) - product(turned, right0, 0, 0)
        right1 = product(inv1, below, 1, 0)
        x1 = product(inv1, right1, 0, 0)
        x1_ref[...] = x1
        x0_ref[...] = product(inv0, right0 - product(turned, x1, 1, 0), 0, 0)

    @pl.when(col == 0)
    def _():
        x0_ref[...] = -inv0.T
        x1_ref[...] = jnp.zeros_like(inv0)

    @pl.when(col == 1)
    def _():
        x0_ref[...] = product(inv0, product(turned, inv1, 1, 1), 0, 0)
        x1_ref[...] = -inv1.T


def final_kernel(mine_ref, own_ref, other0_ref, other_ref, x0_ref, x1_ref, out_ref):
    row = lax.axis_index("row")
    col = lax.axis_index("col")
    core0 = lax.rem(col, 2) == 0
    rows_in = lax.broadcasted_iota(jnp.int32, (NB, NB), 0)
    cols_in = lax.broadcasted_iota(jnp.int32, (NB, NB), 1)
    x_own = jnp.where(core0, x0_ref[...], x1_ref[...])
    x_other = jnp.where(core0, x1_ref[...], x0_ref[...])
    for block in range(2):
        place = pl.ds(block * NB, NB)
        label = row + 16 * block
        other = other0_ref[place, :] + other_ref[place, :]
        taken = product(own_ref[place, :], x_own, 1, 0) + product(other, x_other, 1, 0)
        value = jnp.where(col >= 2, mine_ref[place, :], 0.0) - taken
        last = jnp.minimum(col, 2)
        keep = (label > last) | ((label == last) & ((col >= 2) | (rows_in >= cols_in)))
        out_ref[place, :] = jnp.where(keep, value, 0.0)


def call(body, out, *operands, order=(), work=False, flops=0):
    kept = len(operands)
    blocks = [pltpu.VMEM] * kept + [pl.ANY] * len(order)

    def whole(*refs):
        body(*refs[:kept], *refs[kept + len(order) :])

    outs = jax.tree.map(lambda shape: jax.ShapeDtypeStruct(shape, jnp.float32), out, is_leaf=lambda v: type(v[0]) is int)
    return pl.pallas_call(
        whole,
        out_shape=outs,
        in_specs=[pl.BlockSpec(memory_space=space) for space in blocks],
        scratch_shapes=[pltpu.VMEM((NB, 2 * NB), jnp.float32)] if work else [],
        compiler_params=pltpu.CompilerParams(vmem_limit_bytes=VMEM_LIMIT),
        cost_estimate=pl.CostEstimate(flops=flops, bytes_accessed=0, transcendentals=0) if flops else None,
        name=body.__name__,
    )(*operands, *order)


def both_cores(pairs, mirror):
    out = []
    for s, t in pairs:
        out.append((2 * s, 2 * t))
        if mirror:
            s, t = (CHIPS_Z - s) % CHIPS_Z, (CHIPS_Z - t) % CHIPS_Z
        out.append((2 * s + 1, 2 * t + 1))
    return out


def swap_cores(value, chips):
    return lax.ppermute(value, "col", [(2 * z + c, 2 * z + 1 - c) for z in chips for c in (0, 1)])


def scatter_rows(top):
    return lax.all_to_all(top.reshape(16, 16, NB), "row", 0, 0)[:2]


def no_rows(top):
    return jnp.zeros((2, 16, NB), top.dtype)


def along_z(value, pairs, mirror=False):
    return lax.ppermute(value, "col", both_cores(pairs, mirror))


def local(kernel):
    square = (NB, NB)
    top = kernel[:NB]
    ten_us = 10_000_000_000

    height = lax.axis_index("col") // 2
    bottom = height == 0
    first = lax.cond(bottom, scatter_rows, no_rows, top)
    swapped = swap_cores(first, [0])
    lead = call(lead_kernel, (3, 16, NB), first, swapped)
    other0 = swap_cores(call(mask_kernel, kernel.shape, kernel, order=(lead,)), [0])
    sent = [along_z(lead, p) for p in PIECE_TREE[0]]
    waits = (height == 7) | (height == 9)
    early = lax.cond(bottom | waits, lambda t, l: l[:2], lambda t, l: scatter_rows(t), top, lead)
    lead = call(sum_kernel, (3, 16, NB), lead, *sent, order=(early,))

    panel = call(mask_kernel, kernel.shape, kernel, order=(lead,))
    panel = call(sum_kernel, kernel.shape, panel, along_z(panel, PANEL_TREE[0], True))
    late = lax.cond(waits, lambda t, l: scatter_rows(t), lambda t, l: no_rows(t), top, lead)
    sent = [along_z(lead, p) for p in PIECE_TREE[1]]
    spread = call(spread_kernel, (16, 5, 16, NB), early, late, lead, *sent, order=(panel,))
    lead = lax.all_to_all(spread, "row", 0, 0)

    panel = call(sum_kernel, kernel.shape, panel, along_z(panel, PANEL_TREE[1], True), order=(spread,))
    inv0 = call(first_kernel, square, lead, order=(panel,), work=True, flops=ten_us)
    panel = call(sum_kernel, kernel.shape, panel, along_z(panel, PANEL_TREE[2], True), order=(inv0,))
    turned, inv1 = call(
        second_kernel, (square, square), inv0, lead, order=(panel,), work=True, flops=ten_us
    )
    panel = call(sum_kernel, kernel.shape, panel, along_z(panel, PANEL_TREE[3], True), order=(inv1,))
    other = swap_cores(panel, range(1, CHIPS_Z))
    x0, x1 = call(factors_kernel, (square, square), lead, inv0, turned, inv1, order=(panel,))
    return call(final_kernel, kernel.shape, kernel, panel, other0, other, x0, x1)


def solution(mesh):
    return jax.shard_map(
        local, mesh=mesh, in_specs=(P("row", "col"),), out_specs=P("row", "col"), check_vma=False
    )
```

```python
import jax
import jax.numpy as jnp
from jax import lax
from jax.experimental import pallas as pl
from jax.experimental.pallas import tpu as pltpu
from jax.sharding import PartitionSpec as P

NB = 256
BASE = 32
LANES = 128
SUBS = 8
HIGHEST = lax.Precision.HIGHEST
VMEM_LIMIT = 10 * 1024 * 1024

CHIPS_Z = 16
PANEL_TREE = (
    ((0, 7),),
    ((0, 4), (7, 11)),
    ((0, 2), (4, 6), (7, 9), (11, 13)),
    ((0, 15), (2, 1), (4, 3), (6, 5), (7, 8), (9, 10), (11, 12), (13, 14)),
)
PIECE_TREE = (
    (((0, 12),), ((0, 4),), ((0, 8),)),
    (
        tuple((s, s + 1) for s in (0, 4, 8, 12)),
        tuple((s, (s + 15) % 16) for s in (0, 4, 8, 12)),
        tuple((s, s + 2) for s in (0, 4, 8, 12)),
    ),
)


def product(a, b, a_dim, b_dim):
    return lax.dot_general(
        a,
        b,
        (((a_dim,), (b_dim,)), ((), ())),
        precision=HIGHEST,
        preferred_element_type=jnp.float32,
    )


def split(a):
    high = a.astype(jnp.bfloat16)
    return high, (a - high.astype(jnp.float32)).astype(jnp.bfloat16)


def product3(a, b, a_dim, b_dim):
    dims = (((a_dim,), (b_dim,)), ((), ()))
    a_high, a_low = split(a)
    b_high, b_low = split(b)

    def dot(x, y):
        return lax.dot_general(x, y, dims, preferred_element_type=jnp.float32)

    return dot(a_high, b_high) + (dot(a_high, b_low) + dot(a_low, b_high))


def small_inverse(rows, off):
    groups = BASE // SUBS
    lane = lax.broadcasted_iota(jnp.int32, (SUBS, LANES), 1)
    sub = lax.broadcasted_iota(jnp.int32, (SUBS, LANES), 0)
    cols = [[None] * groups for _ in range(BASE)]
    for c in range(BASE):
        for q in range(c // SUBS, groups):
            piece = rows[SUBS * q : SUBS * q + SUBS, off + c : off + c + 1]
            cols[c][q] = jnp.broadcast_to(piece, (SUBS, LANES))
    inv = [jnp.where(lane == sub + (off + SUBS * q), 1.0, 0.0) for q in range(groups)]
    scale = []
    for k in range(BASE):
        qk, rk = divmod(k, SUBS)
        root = lax.rsqrt(jnp.broadcast_to(cols[k][qk][rk : rk + 1], (SUBS, LANES)))
        recip = root * root
        scaled = [None if part is None else part * recip for part in cols[k]]
        for c in range(k + 1, BASE):
            qc, rc = divmod(c, SUBS)
            factor = jnp.broadcast_to(cols[k][qc][rc : rc + 1], (SUBS, LANES))
            for q in range(qc, groups):
                cols[c][q] = cols[c][q] - scaled[q] * factor
        row = jnp.broadcast_to(inv[qk][rk : rk + 1], (SUBS, LANES)) * recip
        for q in range(qk, groups):
            update = cols[k][q] * row
            if q == qk:
                update = jnp.where(sub > rk, update, 0.0)
            inv[q] = inv[q] - update
        scale.append(root)
    out = []
    for q in range(groups):
        factor = scale[SUBS * q]
        for r in range(1, SUBS):
            factor = jnp.where(sub == r, scale[SUBS * q + r], factor)
        out.append(inv[q] * factor)
    return jnp.concatenate(out, axis=0)


def inverse_factor(square, out_ref, work):
    work[...] = square
    for low in range(0, NB, BASE):
        tile = low // LANES * LANES
        off = low - tile
        high = low + BASE
        small = small_inverse(work[low:high, tile : tile + LANES], off)
        block = small[:, off : off + BASE]
        strip = product(block, work[low:high, :], 1, 0)
        lane = lax.broadcasted_iota(jnp.int32, (BASE, LANES), 1)
        own = jnp.where((lane >= off) & (lane < off + BASE), small, strip[:, tile : tile + LANES])
        strip = jnp.concatenate(
            [own if t == tile else strip[:, t : t + LANES] for t in range(0, NB, LANES)], axis=1
        )
        out_ref[low:high, :] = strip
        for first, last in ((high, high + BASE), (high + BASE, NB)):
            if first < last <= NB:
                left = product(work[first:last, low:high], block, 1, 1)
                old = work[first:last, :]
                lanes = lax.broadcasted_iota(jnp.int32, old.shape, 1)
                old = jnp.where((lanes >= low) & (lanes < high), 0.0, old)
                work[first:last, :] = old - product(left, strip, 1, 0)
    rows = lax.broadcasted_iota(jnp.int32, (NB, NB), 0)
    cols = lax.broadcasted_iota(jnp.int32, (NB, NB), 1)
    out_ref[...] = jnp.where(rows >= cols, out_ref[...], 0.0)


def first_kernel(lead_ref, inv_ref, work):
    inverse_factor(lead_ref[:, 0].reshape(NB, NB), inv_ref, work)


def second_kernel(inv0_ref, lead_ref, turned_ref, inv_ref, work):
    turned = product(inv0_ref[...], lead_ref[:, 1].reshape(NB, NB), 1, 0)
    turned_ref[...] = turned
    square = lead_ref[:, 2].reshape(NB, NB) - product(turned, turned, 0, 0)
    inverse_factor(square, inv_ref, work)


def lead_kernel(first_ref, swapped_ref, lead_ref):
    col = lax.axis_index("col")
    bottom = col < 2
    core0 = lax.rem(col, 2) == 0
    first = jnp.where(bottom, first_ref[...], 0.0)
    swapped = jnp.where(bottom, swapped_ref[...], 0.0)
    lead_ref[0] = jnp.where(core0, first[0], swapped[0])
    lead_ref[1] = jnp.where(core0, swapped[0], first[0])
    lead_ref[2] = jnp.where(core0, swapped[1], first[1])


def mask_kernel(value_ref, out_ref):
    out_ref[...] = jnp.where(lax.axis_index("col") < 2, value_ref[...], 0.0)


def sum_kernel(*refs):
    total = refs[0][...]
    for ref in refs[1:-1]:
        total = total + ref[...]
    refs[-1][...] = total


def spread_kernel(early_ref, late_ref, base_ref, a_ref, b_ref, c_ref, out_ref):
    total = base_ref[...] + a_ref[...] + b_ref[...] + c_ref[...]
    pieces = early_ref[...] + late_ref[...]
    for target in range(out_ref.shape[0]):
        out_ref[target, :3] = total
        out_ref[target, 3:] = pieces


def factors_kernel(cols_ref, inv0_ref, turned_ref, inv1_ref, x0_ref, x1_ref):
    col = lax.axis_index("col")
    inv0 = inv0_ref[...]
    turned = turned_ref[...]
    inv1 = inv1_ref[...]

    @pl.when(col >= 2)
    def _():
        right0 = product3(inv0, cols_ref[:, 3].reshape(NB, NB), 1, 0)
        below = cols_ref[:, 4].reshape(NB, NB) - product3(turned, right0, 0, 0)
        x1 = product3(inv1, product3(inv1, below, 1, 0), 0, 0)
        x1_ref[...] = x1
        x0_ref[...] = product3(inv0, right0 - product3(turned, x1, 1, 0), 0, 0)

    @pl.when(col == 0)
    def _():
        x0_ref[...] = -inv0.T
        x1_ref[...] = jnp.zeros_like(inv0)

    @pl.when(col == 1)
    def _():
        x0_ref[...] = product(inv0, product(turned, inv1, 1, 1), 0, 0)
        x1_ref[...] = -inv1.T


def final_kernel(mine_ref, own_ref, other0_ref, other_ref, x0_ref, x1_ref, out_ref):
    row = lax.axis_index("row")
    col = lax.axis_index("col")
    core0 = lax.rem(col, 2) == 0
    x_own = jnp.where(core0, x0_ref[...], x1_ref[...])
    x_other = jnp.where(core0, x1_ref[...], x0_ref[...])

    @pl.when(col >= 2)
    def _():
        for block in range(2):
            place = pl.ds(block * NB, NB)
            taken = product3(own_ref[place, :], x_own, 1, 0) + product3(other_ref[place, :], x_other, 1, 0)
            out_ref[place, :] = jnp.where(row + 16 * block >= 2, mine_ref[place, :] - taken, 0.0)

    @pl.when(col < 2)
    def _():
        lower = lax.broadcasted_iota(jnp.int32, (NB, NB), 0) >= lax.broadcasted_iota(jnp.int32, (NB, NB), 1)
        for block in range(2):
            place = pl.ds(block * NB, NB)
            label = row + 16 * block
            taken = product(own_ref[place, :], x_own, 1, 0) + product(other0_ref[place, :], x_other, 1, 0)
            out_ref[place, :] = jnp.where((label > col) | ((label == col) & lower), -taken, 0.0)


def call(body, out, *operands, order=(), work=False, flops=0):
    kept = len(operands)
    blocks = [pltpu.VMEM] * kept + [pl.ANY] * len(order)

    def whole(*refs):
        body(*refs[:kept], *refs[kept + len(order) :])

    outs = jax.tree.map(lambda shape: jax.ShapeDtypeStruct(shape, jnp.float32), out, is_leaf=lambda v: type(v[0]) is int)
    return pl.pallas_call(
        whole,
        out_shape=outs,
        in_specs=[pl.BlockSpec(memory_space=space) for space in blocks],
        scratch_shapes=[pltpu.VMEM((NB, NB), jnp.float32)] if work else [],
        compiler_params=pltpu.CompilerParams(vmem_limit_bytes=VMEM_LIMIT),
        cost_estimate=pl.CostEstimate(flops=flops, bytes_accessed=0, transcendentals=0) if flops else None,
        name=body.__name__,
    )(*operands, *order)


def both_cores(pairs, mirror):
    out = []
    for s, t in pairs:
        out.append((2 * s, 2 * t))
        if mirror:
            s, t = (CHIPS_Z - s) % CHIPS_Z, (CHIPS_Z - t) % CHIPS_Z
        out.append((2 * s + 1, 2 * t + 1))
    return out


def swap_cores(value, chips):
    return lax.ppermute(value, "col", [(2 * z + c, 2 * z + 1 - c) for z in chips for c in (0, 1)])


def scatter_rows(top):
    return lax.all_to_all(top.reshape(16, 16, NB), "row", 0, 0)[:2]


def no_rows(top):
    return jnp.zeros((2, 16, NB), top.dtype)


def along_z(value, pairs, mirror=False):
    return lax.ppermute(value, "col", both_cores(pairs, mirror))


def local(kernel):
    square = (NB, NB)
    top = kernel[:NB]
    ten_us = 10_000_000_000

    height = lax.axis_index("col") // 2
    bottom = height == 0
    first = lax.cond(bottom, scatter_rows, no_rows, top)
    swapped = swap_cores(first, [0])
    lead = call(lead_kernel, (3, 16, NB), first, swapped)
    other0 = swap_cores(call(mask_kernel, kernel.shape, kernel, order=(lead,)), [0])
    sent = [along_z(lead, p) for p in PIECE_TREE[0]]
    waits = (height == 7) | (height == 9)
    early = lax.cond(bottom | waits, lambda t, l: l[:2], lambda t, l: scatter_rows(t), top, lead)
    lead = call(sum_kernel, (3, 16, NB), lead, *sent, order=(early,))

    panel = call(mask_kernel, kernel.shape, kernel, order=(lead,))
    panel = call(sum_kernel, kernel.shape, panel, along_z(panel, PANEL_TREE[0], True))
    late = lax.cond(waits, lambda t, l: scatter_rows(t), lambda t, l: no_rows(t), top, lead)
    sent = [along_z(lead, p) for p in PIECE_TREE[1]]
    spread = call(spread_kernel, (16, 5, 16, NB), early, late, lead, *sent, order=(panel,))
    lead = lax.all_to_all(spread, "row", 0, 0)

    panel = call(sum_kernel, kernel.shape, panel, along_z(panel, PANEL_TREE[1], True), order=(spread,))
    inv0 = call(first_kernel, square, lead, order=(panel,), work=True, flops=ten_us)
    panel = call(sum_kernel, kernel.shape, panel, along_z(panel, PANEL_TREE[2], True), order=(inv0,))
    turned, inv1 = call(
        second_kernel, (square, square), inv0, lead, order=(panel,), work=True, flops=ten_us
    )
    panel = call(sum_kernel, kernel.shape, panel, along_z(panel, PANEL_TREE[3], True), order=(inv1,))
    other = swap_cores(panel, range(1, CHIPS_Z))
    x0, x1 = call(factors_kernel, (square, square), lead, inv0, turned, inv1, order=(panel,))
    return call(final_kernel, kernel.shape, kernel, panel, other0, other, x0, x1)


def solution(mesh):
    return jax.shard_map(
        local, mesh=mesh, in_specs=(P("row", "col"),), out_specs=P("row", "col"), check_vma=False
    )
```

```python
import jax
import jax.numpy as jnp
from jax import lax
from jax.experimental import pallas as pl
from jax.experimental.pallas import tpu as pltpu
from jax.sharding import PartitionSpec as P

NB = 256
BASE = 32
LANES = 128
SUBS = 8
HIGHEST = lax.Precision.HIGHEST
VMEM_LIMIT = 6 * 1024 * 1024

CHIPS_Z = 16
PANEL_TREE = (
    ((0, 7),),
    ((0, 4), (7, 11)),
    ((0, 2), (4, 6), (7, 9), (11, 13)),
    ((0, 15), (2, 1), (4, 3), (6, 5), (7, 8), (9, 10), (11, 12), (13, 14)),
)
PIECE_TREE = (
    (((0, 12),), ((0, 4),), ((0, 8),)),
    (
        tuple((s, s + 1) for s in (0, 4, 8, 12)),
        tuple((s, (s + 15) % 16) for s in (0, 4, 8, 12)),
        tuple((s, s + 2) for s in (0, 4, 8, 12)),
    ),
)


def product(a, b, a_dim, b_dim):
    return lax.dot_general(
        a,
        b,
        (((a_dim,), (b_dim,)), ((), ())),
        precision=HIGHEST,
        preferred_element_type=jnp.float32,
    )


def split(a):
    high = a.astype(jnp.bfloat16)
    return high, (a - high.astype(jnp.float32)).astype(jnp.bfloat16)


def product3(a, b, a_dim, b_dim):
    dims = (((a_dim,), (b_dim,)), ((), ()))
    a_high, a_low = split(a)
    b_high, b_low = split(b)

    def dot(x, y):
        return lax.dot_general(x, y, dims, preferred_element_type=jnp.float32)

    return dot(a_high, b_high) + (dot(a_high, b_low) + dot(a_low, b_high))


def small_inverse(rows, off):
    groups = BASE // SUBS
    lane = lax.broadcasted_iota(jnp.int32, (SUBS, LANES), 1)
    sub = lax.broadcasted_iota(jnp.int32, (SUBS, LANES), 0)
    cols = [[None] * groups for _ in range(BASE)]
    for c in range(BASE):
        for q in range(c // SUBS, groups):
            piece = rows[SUBS * q : SUBS * q + SUBS, off + c : off + c + 1]
            cols[c][q] = jnp.broadcast_to(piece, (SUBS, LANES))
    inv = [jnp.where(lane == sub + (off + SUBS * q), 1.0, 0.0) for q in range(groups)]
    scale = []
    for k in range(BASE):
        qk, rk = divmod(k, SUBS)
        root = lax.rsqrt(jnp.broadcast_to(cols[k][qk][rk : rk + 1], (SUBS, LANES)))
        recip = root * root
        scaled = [None if part is None else part * recip for part in cols[k]]
        for c in range(k + 1, BASE):
            qc, rc = divmod(c, SUBS)
            factor = jnp.broadcast_to(cols[k][qc][rc : rc + 1], (SUBS, LANES))
            for q in range(qc, groups):
                cols[c][q] = cols[c][q] - scaled[q] * factor
        row = jnp.broadcast_to(inv[qk][rk : rk + 1], (SUBS, LANES)) * recip
        for q in range(qk, groups):
            update = cols[k][q] * row
            if q == qk:
                update = jnp.where(sub > rk, update, 0.0)
            inv[q] = inv[q] - update
        scale.append(root)
    out = []
    for q in range(groups):
        factor = scale[SUBS * q]
        for r in range(1, SUBS):
            factor = jnp.where(sub == r, scale[SUBS * q + r], factor)
        out.append(inv[q] * factor)
    return jnp.concatenate(out, axis=0)


def inverse_factor(square, out_ref, work):
    work[...] = square
    for low in range(0, NB, BASE):
        tile = low // LANES * LANES
        off = low - tile
        high = low + BASE
        small = small_inverse(work[low:high, tile : tile + LANES], off)
        block = small[:, off : off + BASE]
        strip = product(block, work[low:high, :], 1, 0)
        lane = lax.broadcasted_iota(jnp.int32, (BASE, LANES), 1)
        own = jnp.where((lane >= off) & (lane < off + BASE), small, strip[:, tile : tile + LANES])
        strip = jnp.concatenate(
            [own if t == tile else strip[:, t : t + LANES] for t in range(0, NB, LANES)], axis=1
        )
        out_ref[low:high, :] = strip
        for first, last in ((high, high + BASE), (high + BASE, NB)):
            if first < last <= NB:
                left = product(work[first:last, low:high], block, 1, 1)
                old = work[first:last, :]
                lanes = lax.broadcasted_iota(jnp.int32, old.shape, 1)
                old = jnp.where((lanes >= low) & (lanes < high), 0.0, old)
                work[first:last, :] = old - product(left, strip, 1, 0)
    rows = lax.broadcasted_iota(jnp.int32, (NB, NB), 0)
    cols = lax.broadcasted_iota(jnp.int32, (NB, NB), 1)
    out_ref[...] = jnp.where(rows >= cols, out_ref[...], 0.0)


def first_kernel(lead_ref, inv_ref, work):
    inverse_factor(lead_ref[:, 0].reshape(NB, NB), inv_ref, work)


def second_kernel(inv0_ref, lead_ref, swapped_ref, turned_ref, inv_ref, work):
    core0 = lax.rem(lax.axis_index("col"), 2) == 0
    mine = lead_ref[:, 1].reshape(NB, NB)
    swapped = swapped_ref[...].reshape(NB, NB)
    turned = product(inv0_ref[...], jnp.where(core0, mine, swapped), 1, 1)
    turned_ref[...] = turned
    square = jnp.where(core0, swapped, mine)
    inverse_factor(square - product(turned, turned, 0, 0), inv_ref, work)


def lead_kernel(first_ref, passed_ref, lead_ref):
    core0 = lax.rem(lax.axis_index("col"), 2) == 0
    lead_ref[0] = jnp.where(core0, first_ref[0], passed_ref[...])
    lead_ref[1] = first_ref[1]


def pick_kernel(lead_ref, out_ref):
    out_ref[...] = lead_ref[:, 1]


def panel_kernel(value_ref, panel_ref, mine_ref):
    panel_ref[...] = jnp.where(lax.axis_index("col") < 2, value_ref[...], 0.0)
    mine_ref[...] = value_ref[...]


def sum_kernel(*refs):
    total = refs[0][...]
    for ref in refs[1:-1]:
        total = total + ref[...]
    refs[-1][...] = total


def spread_kernel(early_ref, late_ref, base_ref, a_ref, b_ref, c_ref, out_ref):
    total = base_ref[...] + a_ref[...] + b_ref[...] + c_ref[...]
    pieces = early_ref[...] + late_ref[...]
    for target in range(out_ref.shape[0]):
        out_ref[target, :2] = total
        out_ref[target, 2:] = pieces


def factors_kernel(cols_ref, inv0_ref, turned_ref, inv1_ref, x0_ref, x1_ref):
    col = lax.axis_index("col")
    inv0 = inv0_ref[...]
    turned = turned_ref[...]
    inv1 = inv1_ref[...]

    @pl.when(col >= 2)
    def _():
        right0 = product3(inv0, cols_ref[:, 2].reshape(NB, NB), 1, 0)
        below = cols_ref[:, 3].reshape(NB, NB) - product3(turned, right0, 0, 0)
        x1 = product3(inv1, product3(inv1, below, 1, 0), 0, 0)
        x1_ref[...] = x1
        x0_ref[...] = product3(inv0, right0 - product3(turned, x1, 1, 0), 0, 0)

    @pl.when(col == 0)
    def _():
        x0_ref[...] = -inv0.T
        x1_ref[...] = jnp.zeros_like(inv0)

    @pl.when(col == 1)
    def _():
        x0_ref[...] = product(inv0, product(turned, inv1, 1, 1), 0, 0)
        x1_ref[...] = -inv1.T


def final_kernel(mine_ref, own_ref, other_ref, x0_ref, x1_ref, other0_ref, out_ref, held, sem):
    row = lax.axis_index("row")
    col = lax.axis_index("col")
    core0 = lax.rem(col, 2) == 0
    x_own = jnp.where(core0, x0_ref[...], x1_ref[...])
    x_other = jnp.where(core0, x1_ref[...], x0_ref[...])

    @pl.when(col >= 2)
    def _():
        for block in range(2):
            place = pl.ds(block * NB, NB)
            taken = product(own_ref[place, :], x_own, 1, 0) + product(other_ref[place, :], x_other, 1, 0)
            out_ref[place, :] = jnp.where(row + 16 * block >= 2, mine_ref[place, :] - taken, 0.0)

    @pl.when(col < 2)
    def _():
        copy = pltpu.make_async_copy(other0_ref, held, sem)
        copy.start()
        copy.wait()
        lower = lax.broadcasted_iota(jnp.int32, (NB, NB), 0) >= lax.broadcasted_iota(jnp.int32, (NB, NB), 1)
        for block in range(2):
            place = pl.ds(block * NB, NB)
            label = row + 16 * block
            taken = product(own_ref[place, :], x_own, 1, 0) + product(held[place, :], x_other, 1, 0)
            out_ref[place, :] = jnp.where((label > col) | ((label == col) & lower), -taken, 0.0)


def call(body, out, *operands, far=(), order=(), work=False, flops=0):
    kept = len(operands)
    read = kept + len(far)
    blocks = [pltpu.VMEM] * kept + [pl.ANY] * (len(far) + len(order))
    scratch = [pltpu.VMEM((NB, NB), jnp.float32)] if work else []
    for array in far:
        scratch += [pltpu.VMEM(array.shape, array.dtype), pltpu.SemaphoreType.DMA]

    def whole(*refs):
        body(*refs[:read], *refs[read + len(order) :])

    outs = jax.tree.map(lambda shape: jax.ShapeDtypeStruct(shape, jnp.float32), out, is_leaf=lambda v: type(v[0]) is int)
    return pl.pallas_call(
        whole,
        out_shape=outs,
        in_specs=[pl.BlockSpec(memory_space=space) for space in blocks],
        scratch_shapes=scratch,
        compiler_params=pltpu.CompilerParams(vmem_limit_bytes=VMEM_LIMIT),
        cost_estimate=pl.CostEstimate(flops=flops, bytes_accessed=0, transcendentals=0) if flops else None,
        name=body.__name__,
    )(*operands, *far, *order)


def both_cores(pairs, mirror):
    out = []
    for s, t in pairs:
        out.append((2 * s, 2 * t))
        if mirror:
            s, t = (CHIPS_Z - s) % CHIPS_Z, (CHIPS_Z - t) % CHIPS_Z
        out.append((2 * s + 1, 2 * t + 1))
    return out


def swap_cores(value, chips):
    return lax.ppermute(value, "col", [(2 * z + c, 2 * z + 1 - c) for z in chips for c in (0, 1)])


def scatter_rows(top):
    return lax.all_to_all(top.reshape(16, 16, NB), "row", 0, 0)[:2]


def no_rows(top):
    return jnp.zeros((2, 16, NB), top.dtype)


def along_z(value, pairs, mirror=False):
    return lax.ppermute(value, "col", both_cores(pairs, mirror))


def local(kernel):
    square = (NB, NB)
    top = kernel[:NB]
    ten_us = 10_000_000_000

    height = lax.axis_index("col") // 2
    bottom = height == 0
    first = lax.cond(bottom, scatter_rows, no_rows, top)
    lead = call(lead_kernel, (2, 16, NB), first, lax.ppermute(first[0], "col", [(0, 1)]))
    sent = [along_z(lead, p) for p in PIECE_TREE[0]]
    waits = (height == 7) | (height == 9)
    early = lax.cond(bottom | waits, lambda t, l: l, lambda t, l: scatter_rows(t), top, lead)
    lead = call(sum_kernel, (2, 16, NB), lead, *sent, order=(early,))

    panel, mine = call(panel_kernel, (kernel.shape, kernel.shape), kernel, order=(lead,))
    other0 = swap_cores(mine, [0])
    panel = call(sum_kernel, kernel.shape, panel, along_z(panel, PANEL_TREE[0], True))
    late = lax.cond(waits, lambda t, l: scatter_rows(t), lambda t, l: no_rows(t), top, lead)
    sent = [along_z(lead, p) for p in PIECE_TREE[1]]
    spread = call(spread_kernel, (16, 4, 16, NB), early, late, lead, *sent, order=(panel,))
    lead = lax.all_to_all(spread, "row", 0, 0)
    panel = call(sum_kernel, kernel.shape, panel, along_z(panel, PANEL_TREE[1], True), order=(spread,))
    swapped = swap_cores(call(pick_kernel, (16, 16, NB), lead, order=(panel,)), range(CHIPS_Z))
    inv0 = call(first_kernel, square, lead, order=(panel, other0), work=True, flops=ten_us)
    panel = call(sum_kernel, kernel.shape, panel, along_z(panel, PANEL_TREE[2], True), order=(inv0,))
    turned, inv1 = call(
        second_kernel, (square, square), inv0, lead, swapped, order=(panel,), work=True, flops=ten_us
    )
    panel = call(sum_kernel, kernel.shape, panel, along_z(panel, PANEL_TREE[3], True), order=(inv1,))
    other = swap_cores(panel, range(1, CHIPS_Z))
    x0, x1 = call(factors_kernel, (square, square), lead, inv0, turned, inv1, order=(panel,))
    return call(final_kernel, kernel.shape, mine, panel, other, x0, x1, far=(other0,))


def solution(mesh):
    return jax.shard_map(
        local, mesh=mesh, in_specs=(P("row", "col"),), out_specs=P("row", "col"), check_vma=False
    )
```

```python
import jax
import jax.numpy as jnp
from jax import lax
from jax.experimental import pallas as pl
from jax.experimental.pallas import tpu as pltpu
from jax.sharding import PartitionSpec as P

NB = 256
BASE = 32
LANES = 128
SUBS = 8
HIGHEST = lax.Precision.HIGHEST
VMEM_LIMIT = 6 * 1024 * 1024

CHIPS_Z = 16
PANEL_TREE = (
    ((0, 7),),
    ((0, 4), (7, 11)),
    ((0, 2), (4, 6), (7, 9), (11, 13)),
    ((0, 15), (2, 1), (4, 3), (6, 5), (7, 8), (9, 10), (11, 12), (13, 14)),
)
PIECE_TREE = (
    (((0, 12),), ((0, 4),), ((0, 8),)),
    (
        tuple((s, s + 1) for s in (0, 4, 8, 12)),
        tuple((s, (s + 15) % 16) for s in (0, 4, 8, 12)),
        tuple((s, s + 2) for s in (0, 4, 8, 12)),
    ),
)


def product(a, b, a_dim, b_dim):
    return lax.dot_general(
        a,
        b,
        (((a_dim,), (b_dim,)), ((), ())),
        precision=HIGHEST,
        preferred_element_type=jnp.float32,
    )


def split(a):
    high = a.astype(jnp.bfloat16)
    return high, (a - high.astype(jnp.float32)).astype(jnp.bfloat16)


def product3(a, b, a_dim, b_dim):
    dims = (((a_dim,), (b_dim,)), ((), ()))
    a_high, a_low = split(a)
    b_high, b_low = split(b)

    def dot(x, y):
        return lax.dot_general(x, y, dims, preferred_element_type=jnp.float32)

    return dot(a_high, b_high) + (dot(a_high, b_low) + dot(a_low, b_high))


def small_inverse(rows, off):
    groups = BASE // SUBS
    lane = lax.broadcasted_iota(jnp.int32, (SUBS, LANES), 1)
    sub = lax.broadcasted_iota(jnp.int32, (SUBS, LANES), 0)
    cols = [[None] * groups for _ in range(BASE)]
    for c in range(BASE):
        for q in range(c // SUBS, groups):
            piece = rows[SUBS * q : SUBS * q + SUBS, off + c : off + c + 1]
            cols[c][q] = jnp.broadcast_to(piece, (SUBS, LANES))
    inv = [jnp.where(lane == sub + (off + SUBS * q), 1.0, 0.0) for q in range(groups)]
    scale = []
    for k in range(BASE):
        qk, rk = divmod(k, SUBS)
        root = lax.rsqrt(jnp.broadcast_to(cols[k][qk][rk : rk + 1], (SUBS, LANES)))
        recip = root * root
        scaled = [None if part is None else part * recip for part in cols[k]]
        for c in range(k + 1, BASE):
            qc, rc = divmod(c, SUBS)
            factor = jnp.broadcast_to(cols[k][qc][rc : rc + 1], (SUBS, LANES))
            for q in range(qc, groups):
                cols[c][q] = cols[c][q] - scaled[q] * factor
        row = jnp.broadcast_to(inv[qk][rk : rk + 1], (SUBS, LANES)) * recip
        for q in range(qk, groups):
            update = cols[k][q] * row
            if q == qk:
                update = jnp.where(sub > rk, update, 0.0)
            inv[q] = inv[q] - update
        scale.append(root)
    out = []
    for q in range(groups):
        factor = scale[SUBS * q]
        for r in range(1, SUBS):
            factor = jnp.where(sub == r, scale[SUBS * q + r], factor)
        out.append(inv[q] * factor)
    return jnp.concatenate(out, axis=0)


def inverse_factor(square, out_ref, work):
    work[...] = square
    for low in range(0, NB, BASE):
        tile = low // LANES * LANES
        off = low - tile
        high = low + BASE
        small = small_inverse(work[low:high, tile : tile + LANES], off)
        block = small[:, off : off + BASE]
        strip = product3(block, work[low:high, :], 1, 0)
        lane = lax.broadcasted_iota(jnp.int32, (BASE, LANES), 1)
        own = jnp.where((lane >= off) & (lane < off + BASE), small, strip[:, tile : tile + LANES])
        strip = jnp.concatenate(
            [own if t == tile else strip[:, t : t + LANES] for t in range(0, NB, LANES)], axis=1
        )
        out_ref[low:high, :] = strip
        for first, last in ((high, high + BASE), (high + BASE, NB)):
            if first < last <= NB:
                left = product3(work[first:last, low:high], block, 1, 1)
                old = work[first:last, :]
                lanes = lax.broadcasted_iota(jnp.int32, old.shape, 1)
                old = jnp.where((lanes >= low) & (lanes < high), 0.0, old)
                work[first:last, :] = old - product3(left, strip, 1, 0)
    rows = lax.broadcasted_iota(jnp.int32, (NB, NB), 0)
    cols = lax.broadcasted_iota(jnp.int32, (NB, NB), 1)
    out_ref[...] = jnp.where(rows >= cols, out_ref[...], 0.0)


def first_kernel(lead_ref, inv_ref, work):
    inverse_factor(lead_ref[:, 0].reshape(NB, NB), inv_ref, work)


def second_kernel(inv0_ref, lead_ref, swapped_ref, turned_ref, right_ref, below_ref, inv_ref, work):
    core0 = lax.rem(lax.axis_index("col"), 2) == 0
    mine = lead_ref[:, 1].reshape(NB, NB)
    swapped = swapped_ref[...].reshape(NB, NB)
    inv0 = inv0_ref[...]
    turned = product3(inv0, jnp.where(core0, mine, swapped), 1, 1)
    turned_ref[...] = turned
    square = jnp.where(core0, swapped, mine) - product3(turned, turned, 0, 0)
    right = product3(inv0, lead_ref[:, 2].reshape(NB, NB), 1, 0)
    right_ref[...] = right
    below_ref[...] = lead_ref[:, 3].reshape(NB, NB) - product3(turned, right, 0, 0)
    inverse_factor(square, inv_ref, work)


def lead_kernel(first_ref, passed_ref, lead_ref):
    core0 = lax.rem(lax.axis_index("col"), 2) == 0
    lead_ref[0] = jnp.where(core0, first_ref[0], passed_ref[...])
    lead_ref[1] = first_ref[1]


def pick_kernel(lead_ref, out_ref):
    out_ref[...] = lead_ref[:, 1]


def panel_kernel(value_ref, panel_ref, mine_ref):
    panel_ref[...] = jnp.where(lax.axis_index("col") < 2, value_ref[...], 0.0)
    mine_ref[...] = value_ref[...]


def sum_kernel(*refs):
    total = refs[0][...]
    for ref in refs[1:-1]:
        total = total + ref[...]
    refs[-1][...] = total


def spread_kernel(early_ref, late_ref, base_ref, a_ref, b_ref, c_ref, out_ref):
    total = base_ref[...] + a_ref[...] + b_ref[...] + c_ref[...]
    pieces = early_ref[...] + late_ref[...]
    for target in range(out_ref.shape[0]):
        out_ref[target, :2] = total
        out_ref[target, 2:] = pieces


def factors_kernel(right_ref, below_ref, inv0_ref, turned_ref, inv1_ref, x0_ref, x1_ref):
    col = lax.axis_index("col")
    inv0 = inv0_ref[...]
    turned = turned_ref[...]
    inv1 = inv1_ref[...]

    @pl.when(col >= 2)
    def _():
        x1 = product3(inv1, product3(inv1, below_ref[...], 1, 0), 0, 0)
        x1_ref[...] = x1
        x0_ref[...] = product3(inv0, right_ref[...] - product3(turned, x1, 1, 0), 0, 0)

    @pl.when(col == 0)
    def _():
        x0_ref[...] = -inv0.T
        x1_ref[...] = jnp.zeros_like(inv0)

    @pl.when(col == 1)
    def _():
        x0_ref[...] = product(inv0, product(turned, inv1, 1, 1), 0, 0)
        x1_ref[...] = -inv1.T


def final_kernel(mine_ref, own_ref, other_ref, x0_ref, x1_ref, other0_ref, out_ref, held, sem):
    row = lax.axis_index("row")
    col = lax.axis_index("col")
    core0 = lax.rem(col, 2) == 0
    x_own = jnp.where(core0, x0_ref[...], x1_ref[...])
    x_other = jnp.where(core0, x1_ref[...], x0_ref[...])

    @pl.when(col >= 2)
    def _():
        for block in range(2):
            place = pl.ds(block * NB, NB)
            taken = product(own_ref[place, :], x_own, 1, 0) + product(other_ref[place, :], x_other, 1, 0)
            out_ref[place, :] = jnp.where(row + 16 * block >= 2, mine_ref[place, :] - taken, 0.0)

    @pl.when(col < 2)
    def _():
        copy = pltpu.make_async_copy(other0_ref, held, sem)
        copy.start()
        copy.wait()
        lower = lax.broadcasted_iota(jnp.int32, (NB, NB), 0) >= lax.broadcasted_iota(jnp.int32, (NB, NB), 1)
        for block in range(2):
            place = pl.ds(block * NB, NB)
            label = row + 16 * block
            taken = product(own_ref[place, :], x_own, 1, 0) + product(held[place, :], x_other, 1, 0)
            out_ref[place, :] = jnp.where((label > col) | ((label == col) & lower), -taken, 0.0)


def call(body, out, *operands, far=(), order=(), work=False, flops=0):
    kept = len(operands)
    read = kept + len(far)
    blocks = [pltpu.VMEM] * kept + [pl.ANY] * (len(far) + len(order))
    scratch = [pltpu.VMEM((NB, NB), jnp.float32)] if work else []
    for array in far:
        scratch += [pltpu.VMEM(array.shape, array.dtype), pltpu.SemaphoreType.DMA]

    def whole(*refs):
        body(*refs[:read], *refs[read + len(order) :])

    outs = jax.tree.map(lambda shape: jax.ShapeDtypeStruct(shape, jnp.float32), out, is_leaf=lambda v: type(v[0]) is int)
    return pl.pallas_call(
        whole,
        out_shape=outs,
        in_specs=[pl.BlockSpec(memory_space=space) for space in blocks],
        scratch_shapes=scratch,
        compiler_params=pltpu.CompilerParams(vmem_limit_bytes=VMEM_LIMIT),
        cost_estimate=pl.CostEstimate(flops=flops, bytes_accessed=0, transcendentals=0) if flops else None,
        name=body.__name__,
    )(*operands, *far, *order)


def both_cores(pairs, mirror):
    out = []
    for s, t in pairs:
        out.append((2 * s, 2 * t))
        if mirror:
            s, t = (CHIPS_Z - s) % CHIPS_Z, (CHIPS_Z - t) % CHIPS_Z
        out.append((2 * s + 1, 2 * t + 1))
    return out


def swap_cores(value, chips):
    return lax.ppermute(value, "col", [(2 * z + c, 2 * z + 1 - c) for z in chips for c in (0, 1)])


def scatter_rows(top):
    return lax.all_to_all(top.reshape(16, 16, NB), "row", 0, 0)[:2]


def no_rows(top):
    return jnp.zeros((2, 16, NB), top.dtype)


def along_z(value, pairs, mirror=False):
    return lax.ppermute(value, "col", both_cores(pairs, mirror))


def local(kernel):
    square = (NB, NB)
    top = kernel[:NB]
    ten_us = 10_000_000_000

    height = lax.axis_index("col") // 2
    bottom = height == 0
    first = lax.cond(bottom, scatter_rows, no_rows, top)
    lead = call(lead_kernel, (2, 16, NB), first, lax.ppermute(first[0], "col", [(0, 1)]))
    sent = [along_z(lead, p) for p in PIECE_TREE[0]]
    waits = (height == 7) | (height == 9)
    early = lax.cond(bottom | waits, lambda t, l: l, lambda t, l: scatter_rows(t), top, lead)
    lead = call(sum_kernel, (2, 16, NB), lead, *sent, order=(early,))

    panel, mine = call(panel_kernel, (kernel.shape, kernel.shape), kernel, order=(lead,))
    other0 = swap_cores(mine, [0])
    panel = call(sum_kernel, kernel.shape, panel, along_z(panel, PANEL_TREE[0], True))
    late = lax.cond(waits, lambda t, l: scatter_rows(t), lambda t, l: no_rows(t), top, lead)
    sent = [along_z(lead, p) for p in PIECE_TREE[1]]
    spread = call(spread_kernel, (16, 4, 16, NB), early, late, lead, *sent, order=(panel,))
    lead = lax.all_to_all(spread, "row", 0, 0)
    panel = call(sum_kernel, kernel.shape, panel, along_z(panel, PANEL_TREE[1], True), order=(spread,))
    swapped = swap_cores(call(pick_kernel, (16, 16, NB), lead, order=(panel,)), range(CHIPS_Z))
    inv0 = call(first_kernel, square, lead, order=(panel, other0), work=True, flops=ten_us)
    panel = call(sum_kernel, kernel.shape, panel, along_z(panel, PANEL_TREE[2], True), order=(inv0,))
    turned, right, below, inv1 = call(
        second_kernel, (square,) * 4, inv0, lead, swapped, order=(panel,), work=True, flops=ten_us
    )
    panel = call(sum_kernel, kernel.shape, panel, along_z(panel, PANEL_TREE[3], True), order=(inv1,))
    other = swap_cores(panel, range(1, CHIPS_Z))
    x0, x1 = call(factors_kernel, (square, square), right, below, inv0, turned, inv1, order=(panel,))
    return call(final_kernel, kernel.shape, mine, panel, other, x0, x1, far=(other0,))


def solution(mesh):
    return jax.shard_map(
        local, mesh=mesh, in_specs=(P("row", "col"),), out_specs=P("row", "col"), check_vma=False
    )
```

```python
import jax
import jax.numpy as jnp
from jax import lax
from jax.experimental import pallas as pl
from jax.experimental.pallas import tpu as pltpu
from jax.sharding import PartitionSpec as P

NB = 256
BASE = 32
LANES = 128
SUBS = 8
VMEM_LIMIT = 6 * 1024 * 1024

CHIPS_Z = 16
PANEL_TREE = (
    ((0, 7),),
    ((0, 4), (7, 11)),
    ((0, 2), (4, 6), (7, 9), (11, 13)),
    ((0, 15), (2, 1), (4, 3), (6, 5), (7, 8), (9, 10), (11, 12), (13, 14)),
)
PIECE_TREE = (
    (((0, 12),), ((0, 4),), ((0, 8),)),
    (
        tuple((s, s + 1) for s in (0, 4, 8, 12)),
        tuple((s, (s + 15) % 16) for s in (0, 4, 8, 12)),
        tuple((s, s + 2) for s in (0, 4, 8, 12)),
    ),
)


def split(a):
    high = a.astype(jnp.bfloat16)
    return high, (a - high.astype(jnp.float32)).astype(jnp.bfloat16)


def product3(a, b, a_dim, b_dim):
    dims = (((a_dim,), (b_dim,)), ((), ()))
    a_high, a_low = split(a)
    b_high, b_low = split(b)

    def dot(x, y):
        return lax.dot_general(x, y, dims, preferred_element_type=jnp.float32)

    return dot(a_high, b_high) + (dot(a_high, b_low) + dot(a_low, b_high))


def small_inverse(rows, off):
    groups = BASE // SUBS
    lane = lax.broadcasted_iota(jnp.int32, (SUBS, LANES), 1)
    sub = lax.broadcasted_iota(jnp.int32, (SUBS, LANES), 0)
    cols = [[None] * groups for _ in range(BASE)]
    for c in range(BASE):
        for q in range(c // SUBS, groups):
            piece = rows[SUBS * q : SUBS * q + SUBS, off + c : off + c + 1]
            cols[c][q] = jnp.broadcast_to(piece, (SUBS, LANES))
    inv = [jnp.where(lane == sub + (off + SUBS * q), 1.0, 0.0) for q in range(groups)]
    scale = []
    for k in range(BASE):
        qk, rk = divmod(k, SUBS)
        root = lax.rsqrt(jnp.broadcast_to(cols[k][qk][rk : rk + 1], (SUBS, LANES)))
        recip = root * root
        scaled = [None if part is None else part * recip for part in cols[k]]
        for c in range(k + 1, BASE):
            qc, rc = divmod(c, SUBS)
            factor = jnp.broadcast_to(cols[k][qc][rc : rc + 1], (SUBS, LANES))
            for q in range(qc, groups):
                cols[c][q] = cols[c][q] - scaled[q] * factor
        row = jnp.broadcast_to(inv[qk][rk : rk + 1], (SUBS, LANES)) * recip
        for q in range(qk, groups):
            update = cols[k][q] * row
            if q == qk:
                update = jnp.where(sub > rk, update, 0.0)
            inv[q] = inv[q] - update
        scale.append(root)
    out = []
    for q in range(groups):
        factor = scale[SUBS * q]
        for r in range(1, SUBS):
            factor = jnp.where(sub == r, scale[SUBS * q + r], factor)
        out.append(inv[q] * factor)
    return jnp.concatenate(out, axis=0)


def inverse_factor(square, out_ref, work):
    work[...] = square
    for low in range(0, NB, BASE):
        tile = low // LANES * LANES
        off = low - tile
        high = low + BASE
        small = small_inverse(work[low:high, tile : tile + LANES], off)
        block = small[:, off : off + BASE]
        strip = product3(block, work[low:high, :], 1, 0)
        lane = lax.broadcasted_iota(jnp.int32, (BASE, LANES), 1)
        own = jnp.where((lane >= off) & (lane < off + BASE), small, strip[:, tile : tile + LANES])
        strip = jnp.concatenate(
            [own if t == tile else strip[:, t : t + LANES] for t in range(0, NB, LANES)], axis=1
        )
        out_ref[low:high, :] = strip
        for first, last in ((high, high + BASE), (high + BASE, NB)):
            if first < last <= NB:
                left = product3(work[first:last, low:high], block, 1, 1)
                old = work[first:last, :]
                lanes = lax.broadcasted_iota(jnp.int32, old.shape, 1)
                old = jnp.where((lanes >= low) & (lanes < high), 0.0, old)
                work[first:last, :] = old - product3(left, strip, 1, 0)
    rows = lax.broadcasted_iota(jnp.int32, (NB, NB), 0)
    cols = lax.broadcasted_iota(jnp.int32, (NB, NB), 1)
    out_ref[...] = jnp.where(rows >= cols, out_ref[...], 0.0)


def first_kernel(lead_ref, inv_ref, work):
    inverse_factor(lead_ref[:, 0].reshape(NB, NB), inv_ref, work)


def second_kernel(inv0_ref, lead_ref, swapped_ref, turned_ref, right_ref, below_ref, inv_ref, work):
    core0 = lax.rem(lax.axis_index("col"), 2) == 0
    mine = lead_ref[:, 1].reshape(NB, NB)
    swapped = swapped_ref[...].reshape(NB, NB)
    inv0 = inv0_ref[...]
    turned = product3(inv0, jnp.where(core0, mine, swapped), 1, 1)
    turned_ref[...] = turned
    square = jnp.where(core0, swapped, mine) - product3(turned, turned, 0, 0)
    right = product3(inv0, lead_ref[:, 2].reshape(NB, NB), 1, 0)
    right_ref[...] = right
    below_ref[...] = lead_ref[:, 3].reshape(NB, NB) - product3(turned, right, 0, 0)
    inverse_factor(square, inv_ref, work)


def lead_kernel(first_ref, passed_ref, lead_ref):
    core0 = lax.rem(lax.axis_index("col"), 2) == 0
    lead_ref[0] = jnp.where(core0, first_ref[0], passed_ref[...])
    lead_ref[1] = first_ref[1]


def pick_kernel(lead_ref, out_ref):
    out_ref[...] = lead_ref[:, 1]


def panel_kernel(value_ref, panel_ref, mine_ref):
    panel_ref[...] = jnp.where(lax.axis_index("col") < 2, value_ref[...], 0.0)
    mine_ref[...] = value_ref[...]


def sum_kernel(*refs):
    total = refs[0][...]
    for ref in refs[1:-1]:
        total = total + ref[...]
    refs[-1][...] = total


def spread_kernel(early_ref, late_ref, base_ref, a_ref, b_ref, c_ref, out_ref):
    total = base_ref[...] + a_ref[...] + b_ref[...] + c_ref[...]
    pieces = early_ref[...] + late_ref[...]
    for target in range(out_ref.shape[0]):
        out_ref[target, :2] = total
        out_ref[target, 2:] = pieces


def factors_kernel(right_ref, below_ref, inv0_ref, turned_ref, inv1_ref, x0_ref, x1_ref):
    col = lax.axis_index("col")
    inv0 = inv0_ref[...]
    turned = turned_ref[...]
    inv1 = inv1_ref[...]

    @pl.when(col >= 2)
    def _():
        x1 = product3(inv1, product3(inv1, below_ref[...], 1, 0), 0, 0)
        x1_ref[...] = x1
        x0_ref[...] = product3(inv0, right_ref[...] - product3(turned, x1, 1, 0), 0, 0)

    @pl.when(col == 0)
    def _():
        x0_ref[...] = -inv0.T
        x1_ref[...] = jnp.zeros_like(inv0)

    @pl.when(col == 1)
    def _():
        x0_ref[...] = product3(inv0, product3(turned, inv1, 1, 1), 0, 0)
        x1_ref[...] = -inv1.T


def final_kernel(mine_ref, own_ref, other_ref, x0_ref, x1_ref, other0_ref, out_ref, held, sem):
    row = lax.axis_index("row")
    col = lax.axis_index("col")
    core0 = lax.rem(col, 2) == 0
    x_own = jnp.where(core0, x0_ref[...], x1_ref[...])
    x_other = jnp.where(core0, x1_ref[...], x0_ref[...])

    @pl.when(col >= 2)
    def _():
        for block in range(2):
            place = pl.ds(block * NB, NB)
            taken = product3(own_ref[place, :], x_own, 1, 0) + product3(other_ref[place, :], x_other, 1, 0)
            out_ref[place, :] = jnp.where(row + 16 * block >= 2, mine_ref[place, :] - taken, 0.0)

    @pl.when(col < 2)
    def _():
        copy = pltpu.make_async_copy(other0_ref, held, sem)
        copy.start()
        first = product3(own_ref[...], x_own, 1, 0)
        lower = lax.broadcasted_iota(jnp.int32, (NB, NB), 0) >= lax.broadcasted_iota(jnp.int32, (NB, NB), 1)
        copy.wait()
        taken = first + product3(held[...], x_other, 1, 0)
        for block in range(2):
            place = slice(block * NB, block * NB + NB)
            label = row + 16 * block
            out_ref[place, :] = jnp.where((label > col) | ((label == col) & lower), -taken[place, :], 0.0)


def call(body, out, *operands, far=(), order=(), work=False, flops=0):
    kept = len(operands)
    read = kept + len(far)
    blocks = [pltpu.VMEM] * kept + [pl.ANY] * (len(far) + len(order))
    scratch = [pltpu.VMEM((NB, NB), jnp.float32)] if work else []
    for array in far:
        scratch += [pltpu.VMEM(array.shape, array.dtype), pltpu.SemaphoreType.DMA]

    def whole(*refs):
        body(*refs[:read], *refs[read + len(order) :])

    outs = jax.tree.map(lambda shape: jax.ShapeDtypeStruct(shape, jnp.float32), out, is_leaf=lambda v: type(v[0]) is int)
    return pl.pallas_call(
        whole,
        out_shape=outs,
        in_specs=[pl.BlockSpec(memory_space=space) for space in blocks],
        scratch_shapes=scratch,
        compiler_params=pltpu.CompilerParams(vmem_limit_bytes=VMEM_LIMIT),
        cost_estimate=pl.CostEstimate(flops=flops, bytes_accessed=0, transcendentals=0) if flops else None,
        name=body.__name__,
    )(*operands, *far, *order)


def both_cores(pairs, mirror):
    out = []
    for s, t in pairs:
        out.append((2 * s, 2 * t))
        if mirror:
            s, t = (CHIPS_Z - s) % CHIPS_Z, (CHIPS_Z - t) % CHIPS_Z
        out.append((2 * s + 1, 2 * t + 1))
    return out


def swap_cores(value, chips):
    return lax.ppermute(value, "col", [(2 * z + c, 2 * z + 1 - c) for z in chips for c in (0, 1)])


def scatter_rows(top):
    return lax.all_to_all(top.reshape(16, 16, NB), "row", 0, 0)[:2]


def no_rows(top):
    return jnp.zeros((2, 16, NB), top.dtype)


def along_z(value, pairs, mirror=False):
    return lax.ppermute(value, "col", both_cores(pairs, mirror))


def local(kernel):
    square = (NB, NB)
    top = kernel[:NB]
    ten_us = 10_000_000_000

    height = lax.axis_index("col") // 2
    bottom = height == 0
    first = lax.cond(bottom, scatter_rows, no_rows, top)
    lead = call(lead_kernel, (2, 16, NB), first, lax.ppermute(first[0], "col", [(0, 1)]))
    sent = [along_z(lead, p) for p in PIECE_TREE[0]]
    waits = (height == 7) | (height == 9)
    early = lax.cond(bottom | waits, lambda t, l: l, lambda t, l: scatter_rows(t), top, lead)
    lead = call(sum_kernel, (2, 16, NB), lead, *sent, order=(early,))

    panel, mine = call(panel_kernel, (kernel.shape, kernel.shape), kernel, order=(lead,))
    other0 = swap_cores(mine, [0])
    panel = call(sum_kernel, kernel.shape, panel, along_z(panel, PANEL_TREE[0], True))
    late = lax.cond(waits, lambda t, l: scatter_rows(t), lambda t, l: no_rows(t), top, lead)
    sent = [along_z(lead, p) for p in PIECE_TREE[1]]
    spread = call(spread_kernel, (16, 4, 16, NB), early, late, lead, *sent, order=(panel,))
    lead = lax.all_to_all(spread, "row", 0, 0)
    panel = call(sum_kernel, kernel.shape, panel, along_z(panel, PANEL_TREE[1], True), order=(spread,))
    swapped = swap_cores(call(pick_kernel, (16, 16, NB), lead, order=(panel,)), range(CHIPS_Z))
    inv0 = call(first_kernel, square, lead, order=(panel, other0), work=True, flops=ten_us)
    panel = call(sum_kernel, kernel.shape, panel, along_z(panel, PANEL_TREE[2], True), order=(inv0,))
    turned, right, below, inv1 = call(
        second_kernel, (square,) * 4, inv0, lead, swapped, order=(panel,), work=True, flops=ten_us
    )
    panel = call(sum_kernel, kernel.shape, panel, along_z(panel, PANEL_TREE[3], True), order=(inv1,))
    other = swap_cores(panel, range(1, CHIPS_Z))
    x0, x1 = call(factors_kernel, (square, square), right, below, inv0, turned, inv1, order=(panel,))
    return call(final_kernel, kernel.shape, mine, panel, other, x0, x1, far=(other0,))


def solution(mesh):
    return jax.shard_map(
        local, mesh=mesh, in_specs=(P("row", "col"),), out_specs=P("row", "col"), check_vma=False
    )
```

```python
import jax
import jax.numpy as jnp
from jax import lax
from jax.experimental import pallas as pl
from jax.experimental.pallas import tpu as pltpu
from jax.sharding import PartitionSpec as P

NB = 256
BASE = 32
LANES = 128
SUBS = 8
VMEM_LIMIT = 6 * 1024 * 1024

CHIPS_Z = 16
PANEL_TREE = (
    ((0, 7),),
    ((0, 4), (7, 11)),
    ((0, 2), (7, 6), (4, 8), (11, 13)),
    ((0, 15), (2, 1), (4, 3), (6, 5), (7, 10), (8, 9), (11, 12), (13, 14)),
)
PIECE_TREE = (
    (((0, 12),), ((0, 4),), ((0, 8),)),
    (
        tuple((s, s + 1) for s in (0, 4, 8, 12)),
        tuple((s, (s + 15) % 16) for s in (0, 4, 8, 12)),
        tuple((s, s + 2) for s in (0, 4, 8, 12)),
    ),
)


def split(a):
    high = a.astype(jnp.bfloat16)
    return high, (a - high.astype(jnp.float32)).astype(jnp.bfloat16)


def product3(a, b, a_dim, b_dim):
    dims = (((a_dim,), (b_dim,)), ((), ()))
    a_high, a_low = split(a)
    b_high, b_low = split(b)

    def dot(x, y):
        return lax.dot_general(x, y, dims, preferred_element_type=jnp.float32)

    return dot(a_high, b_high) + (dot(a_high, b_low) + dot(a_low, b_high))


def small_inverse(rows, off):
    groups = BASE // SUBS
    lane = lax.broadcasted_iota(jnp.int32, (SUBS, LANES), 1)
    sub = lax.broadcasted_iota(jnp.int32, (SUBS, LANES), 0)
    cols = [[None] * groups for _ in range(BASE)]
    for c in range(BASE):
        for q in range(c // SUBS, groups):
            piece = rows[SUBS * q : SUBS * q + SUBS, off + c : off + c + 1]
            cols[c][q] = jnp.broadcast_to(piece, (SUBS, LANES))
    inv = [jnp.where(lane == sub + (off + SUBS * q), 1.0, 0.0) for q in range(groups)]
    scale = []
    for k in range(BASE):
        qk, rk = divmod(k, SUBS)
        root = lax.rsqrt(jnp.broadcast_to(cols[k][qk][rk : rk + 1], (SUBS, LANES)))
        recip = root * root
        scaled = [None if part is None else part * recip for part in cols[k]]
        for c in range(k + 1, BASE):
            qc, rc = divmod(c, SUBS)
            factor = jnp.broadcast_to(cols[k][qc][rc : rc + 1], (SUBS, LANES))
            for q in range(qc, groups):
                cols[c][q] = cols[c][q] - scaled[q] * factor
        row = jnp.broadcast_to(inv[qk][rk : rk + 1], (SUBS, LANES)) * recip
        for q in range(qk, groups):
            update = cols[k][q] * row
            if q == qk:
                update = jnp.where(sub > rk, update, 0.0)
            inv[q] = inv[q] - update
        scale.append(root)
    out = []
    for q in range(groups):
        factor = scale[SUBS * q]
        for r in range(1, SUBS):
            factor = jnp.where(sub == r, scale[SUBS * q + r], factor)
        out.append(inv[q] * factor)
    return jnp.concatenate(out, axis=0)


def inverse_factor(square, out_ref, work):
    work[...] = square
    for low in range(0, NB, BASE):
        tile = low // LANES * LANES
        off = low - tile
        high = low + BASE
        small = small_inverse(work[low:high, tile : tile + LANES], off)
        block = small[:, off : off + BASE]
        strip = product3(block, work[low:high, :], 1, 0)
        lane = lax.broadcasted_iota(jnp.int32, (BASE, LANES), 1)
        own = jnp.where((lane >= off) & (lane < off + BASE), small, strip[:, tile : tile + LANES])
        strip = jnp.concatenate(
            [own if t == tile else strip[:, t : t + LANES] for t in range(0, NB, LANES)], axis=1
        )
        out_ref[low:high, :] = strip
        for first, last in ((high, high + BASE), (high + BASE, NB)):
            if first < last <= NB:
                left = product3(work[first:last, low:high], block, 1, 1)
                old = work[first:last, :]
                lanes = lax.broadcasted_iota(jnp.int32, old.shape, 1)
                old = jnp.where((lanes >= low) & (lanes < high), 0.0, old)
                work[first:last, :] = old - product3(left, strip, 1, 0)
    rows = lax.broadcasted_iota(jnp.int32, (NB, NB), 0)
    cols = lax.broadcasted_iota(jnp.int32, (NB, NB), 1)
    out_ref[...] = jnp.where(rows >= cols, out_ref[...], 0.0)


def first_kernel(lead_ref, inv_ref, work):
    inverse_factor(lead_ref[:, 0].reshape(NB, NB), inv_ref, work)


def second_kernel(inv0_ref, lead_ref, swapped_ref, turned_ref, right_ref, below_ref, inv_ref, work):
    core0 = lax.rem(lax.axis_index("col"), 2) == 0
    mine = lead_ref[:, 1].reshape(NB, NB)
    swapped = swapped_ref[...].reshape(NB, NB)
    inv0 = inv0_ref[...]
    turned = product3(inv0, jnp.where(core0, mine, swapped), 1, 1)
    turned_ref[...] = turned
    square = jnp.where(core0, swapped, mine) - product3(turned, turned, 0, 0)
    right = product3(inv0, lead_ref[:, 2].reshape(NB, NB), 1, 0)
    right_ref[...] = right
    below_ref[...] = lead_ref[:, 3].reshape(NB, NB) - product3(turned, right, 0, 0)
    inverse_factor(square, inv_ref, work)


def lead_kernel(first_ref, passed_ref, lead_ref):
    core0 = lax.rem(lax.axis_index("col"), 2) == 0
    lead_ref[0] = jnp.where(core0, first_ref[0], passed_ref[...])
    lead_ref[1] = first_ref[1]


def pick_kernel(lead_ref, out_ref):
    out_ref[...] = lead_ref[:, 1]


def panel_kernel(value_ref, panel_ref, mine_ref):
    panel_ref[...] = jnp.where(lax.axis_index("col") < 2, value_ref[...], 0.0)
    mine_ref[...] = value_ref[...]


def sum_kernel(*refs):
    total = refs[0][...]
    for ref in refs[1:-1]:
        total = total + ref[...]
    refs[-1][...] = total


def spread_kernel(early_ref, late_ref, base_ref, a_ref, b_ref, c_ref, out_ref):
    total = base_ref[...] + a_ref[...] + b_ref[...] + c_ref[...]
    pieces = early_ref[...] + late_ref[...]
    for target in range(out_ref.shape[0]):
        out_ref[target, :2] = total
        out_ref[target, 2:] = pieces


def factors_kernel(right_ref, below_ref, inv0_ref, turned_ref, inv1_ref, x0_ref, x1_ref):
    col = lax.axis_index("col")
    inv0 = inv0_ref[...]
    turned = turned_ref[...]
    inv1 = inv1_ref[...]

    @pl.when(col >= 2)
    def _():
        x1 = product3(inv1, product3(inv1, below_ref[...], 1, 0), 0, 0)
        x1_ref[...] = x1
        x0_ref[...] = product3(inv0, right_ref[...] - product3(turned, x1, 1, 0), 0, 0)

    @pl.when(col == 0)
    def _():
        x0_ref[...] = -inv0.T
        x1_ref[...] = jnp.zeros_like(inv0)

    @pl.when(col == 1)
    def _():
        x0_ref[...] = product3(inv0, product3(turned, inv1, 1, 1), 0, 0)
        x1_ref[...] = -inv1.T


def final_kernel(mine_ref, own_ref, other_ref, x0_ref, x1_ref, other0_ref, out_ref, held, sem):
    row = lax.axis_index("row")
    col = lax.axis_index("col")
    core0 = lax.rem(col, 2) == 0
    x_own = jnp.where(core0, x0_ref[...], x1_ref[...])
    x_other = jnp.where(core0, x1_ref[...], x0_ref[...])

    @pl.when(col >= 2)
    def _():
        for block in range(2):
            place = pl.ds(block * NB, NB)
            taken = product3(own_ref[place, :], x_own, 1, 0) + product3(other_ref[place, :], x_other, 1, 0)
            out_ref[place, :] = jnp.where(row + 16 * block >= 2, mine_ref[place, :] - taken, 0.0)

    @pl.when(col < 2)
    def _():
        copy = pltpu.make_async_copy(other0_ref, held, sem)
        copy.start()
        first = product3(own_ref[...], x_own, 1, 0)
        lower = lax.broadcasted_iota(jnp.int32, (NB, NB), 0) >= lax.broadcasted_iota(jnp.int32, (NB, NB), 1)
        copy.wait()
        taken = first + product3(held[...], x_other, 1, 0)
        for block in range(2):
            place = slice(block * NB, block * NB + NB)
            label = row + 16 * block
            out_ref[place, :] = jnp.where((label > col) | ((label == col) & lower), -taken[place, :], 0.0)


def call(body, out, *operands, far=(), order=(), work=False, flops=0):
    kept = len(operands)
    read = kept + len(far)
    blocks = [pltpu.VMEM] * kept + [pl.ANY] * (len(far) + len(order))
    scratch = [pltpu.VMEM((NB, NB), jnp.float32)] if work else []
    for array in far:
        scratch += [pltpu.VMEM(array.shape, array.dtype), pltpu.SemaphoreType.DMA]

    def whole(*refs):
        body(*refs[:read], *refs[read + len(order) :])

    outs = jax.tree.map(lambda shape: jax.ShapeDtypeStruct(shape, jnp.float32), out, is_leaf=lambda v: type(v[0]) is int)
    return pl.pallas_call(
        whole,
        out_shape=outs,
        in_specs=[pl.BlockSpec(memory_space=space) for space in blocks],
        scratch_shapes=scratch,
        compiler_params=pltpu.CompilerParams(vmem_limit_bytes=VMEM_LIMIT),
        cost_estimate=pl.CostEstimate(flops=flops, bytes_accessed=0, transcendentals=0) if flops else None,
        name=body.__name__,
    )(*operands, *far, *order)


def both_cores(pairs, mirror):
    out = []
    for s, t in pairs:
        out.append((2 * s, 2 * t))
        if mirror:
            s, t = (CHIPS_Z - s) % CHIPS_Z, (CHIPS_Z - t) % CHIPS_Z
        out.append((2 * s + 1, 2 * t + 1))
    return out


def swap_cores(value, chips):
    return lax.ppermute(value, "col", [(2 * z + c, 2 * z + 1 - c) for z in chips for c in (0, 1)])


def scatter_rows(top):
    return lax.all_to_all(top.reshape(16, 16, NB), "row", 0, 0)[:2]


def no_rows(top):
    return jnp.zeros((2, 16, NB), top.dtype)


def along_z(value, pairs, mirror=False):
    return lax.ppermute(value, "col", both_cores(pairs, mirror))


def local(kernel):
    square = (NB, NB)
    top = kernel[:NB]
    ten_us = 10_000_000_000

    height = lax.axis_index("col") // 2
    bottom = height == 0
    first = lax.cond(bottom, scatter_rows, no_rows, top)
    lead = call(lead_kernel, (2, 16, NB), first, lax.ppermute(first[0], "col", [(0, 1)]))
    sent = [along_z(lead, p) for p in PIECE_TREE[0]]
    waits = (height == 7) | (height == 9)
    early = lax.cond(bottom | waits, lambda t, l: l, lambda t, l: scatter_rows(t), top, lead)
    lead = call(sum_kernel, (2, 16, NB), lead, *sent, order=(early,))

    panel, mine = call(panel_kernel, (kernel.shape, kernel.shape), kernel, order=(lead,))
    other0 = swap_cores(mine, [0])
    panel = call(sum_kernel, kernel.shape, panel, along_z(panel, PANEL_TREE[0], True))
    late = lax.cond(waits, lambda t, l: scatter_rows(t), lambda t, l: no_rows(t), top, lead)
    sent = [along_z(lead, p) for p in PIECE_TREE[1]]
    spread = call(spread_kernel, (16, 4, 16, NB), early, late, lead, *sent, order=(panel,))
    lead = lax.all_to_all(spread, "row", 0, 0)
    panel = call(sum_kernel, kernel.shape, panel, along_z(panel, PANEL_TREE[1], True), order=(spread,))
    swapped = swap_cores(call(pick_kernel, (16, 16, NB), lead, order=(panel,)), range(CHIPS_Z))
    inv0 = call(first_kernel, square, lead, order=(panel, other0), work=True, flops=ten_us)
    panel = call(sum_kernel, kernel.shape, panel, along_z(panel, PANEL_TREE[2], True), order=(inv0,))
    turned, right, below, inv1 = call(
        second_kernel, (square,) * 4, inv0, lead, swapped, order=(panel,), work=True, flops=ten_us
    )
    panel = call(sum_kernel, kernel.shape, panel, along_z(panel, PANEL_TREE[3], True), order=(inv1,))
    other = swap_cores(panel, range(1, CHIPS_Z))
    x0, x1 = call(factors_kernel, (square, square), right, below, inv0, turned, inv1, order=(panel,))
    return call(final_kernel, kernel.shape, mine, panel, other, x0, x1, far=(other0,))


def solution(mesh):
    return jax.shard_map(
        local, mesh=mesh, in_specs=(P("row", "col"),), out_specs=P("row", "col"), check_vma=False
    )
```

```python
import jax
import jax.numpy as jnp
from jax import lax
from jax.experimental import pallas as pl
from jax.experimental.pallas import tpu as pltpu
from jax.sharding import PartitionSpec as P

NB = 256
BASE = 32
LANES = 128
SUBS = 8
VMEM_LIMIT = 6 * 1024 * 1024

CHIPS_Z = 16
PANEL_TREE = (
    ((0, 7),),
    ((0, 4), (7, 11)),
    ((0, 2), (4, 6), (7, 9), (11, 13)),
    ((0, 15), (2, 1), (4, 3), (6, 5), (7, 8), (9, 10), (11, 12), (13, 14)),
)
PIECE_TREE = (
    (((0, 12),), ((0, 4),), ((0, 8),)),
    (
        tuple((s, s + 1) for s in (0, 4, 8, 12)),
        tuple((s, (s + 15) % 16) for s in (0, 4, 8, 12)),
        tuple((s, s + 2) for s in (0, 4, 8, 12)),
    ),
)


def split(a):
    high = a.astype(jnp.bfloat16)
    return high, (a - high.astype(jnp.float32)).astype(jnp.bfloat16)


def product3(a, b, a_dim, b_dim):
    dims = (((a_dim,), (b_dim,)), ((), ()))
    a_high, a_low = split(a)
    b_high, b_low = split(b)

    def dot(x, y):
        return lax.dot_general(x, y, dims, preferred_element_type=jnp.float32)

    return dot(a_high, b_high) + (dot(a_high, b_low) + dot(a_low, b_high))


def small_inverse(rows, off):
    groups = BASE // SUBS
    lane = lax.broadcasted_iota(jnp.int32, (SUBS, LANES), 1)
    sub = lax.broadcasted_iota(jnp.int32, (SUBS, LANES), 0)
    cols = [[None] * groups for _ in range(BASE)]
    for c in range(BASE):
        for q in range(c // SUBS, groups):
            piece = rows[SUBS * q : SUBS * q + SUBS, off + c : off + c + 1]
            cols[c][q] = jnp.broadcast_to(piece, (SUBS, LANES))
    inv = [jnp.where(lane == sub + (off + SUBS * q), 1.0, 0.0) for q in range(groups)]
    scale = []
    for k in range(BASE):
        qk, rk = divmod(k, SUBS)
        root = lax.rsqrt(jnp.broadcast_to(cols[k][qk][rk : rk + 1], (SUBS, LANES)))
        recip = root * root
        scaled = [None if part is None else part * recip for part in cols[k]]
        for c in range(k + 1, BASE):
            qc, rc = divmod(c, SUBS)
            factor = jnp.broadcast_to(cols[k][qc][rc : rc + 1], (SUBS, LANES))
            for q in range(qc, groups):
                cols[c][q] = cols[c][q] - scaled[q] * factor
        row = jnp.broadcast_to(inv[qk][rk : rk + 1], (SUBS, LANES)) * recip
        for q in range(qk, groups):
            update = cols[k][q] * row
            if q == qk:
                update = jnp.where(sub > rk, update, 0.0)
            inv[q] = inv[q] - update
        scale.append(root)
    out = []
    for q in range(groups):
        factor = scale[SUBS * q]
        for r in range(1, SUBS):
            factor = jnp.where(sub == r, scale[SUBS * q + r], factor)
        out.append(inv[q] * factor)
    return jnp.concatenate(out, axis=0)


def inverse_factor(square, out_ref, work):
    work[...] = square
    for low in range(0, NB, BASE):
        tile = low // LANES * LANES
        off = low - tile
        high = low + BASE
        small = small_inverse(work[low:high, tile : tile + LANES], off)
        block = small[:, off : off + BASE]
        strip = product3(block, work[low:high, :], 1, 0)
        lane = lax.broadcasted_iota(jnp.int32, (BASE, LANES), 1)
        own = jnp.where((lane >= off) & (lane < off + BASE), small, strip[:, tile : tile + LANES])
        strip = jnp.concatenate(
            [own if t == tile else strip[:, t : t + LANES] for t in range(0, NB, LANES)], axis=1
        )
        out_ref[low:high, :] = strip
        for first, last in ((high, high + BASE), (high + BASE, NB)):
            if first < last <= NB:
                left = product3(work[first:last, low:high], block, 1, 1)
                old = work[first:last, :]
                lanes = lax.broadcasted_iota(jnp.int32, old.shape, 1)
                old = jnp.where((lanes >= low) & (lanes < high), 0.0, old)
                work[first:last, :] = old - product3(left, strip, 1, 0)
    rows = lax.broadcasted_iota(jnp.int32, (NB, NB), 0)
    cols = lax.broadcasted_iota(jnp.int32, (NB, NB), 1)
    out_ref[...] = jnp.where(rows >= cols, out_ref[...], 0.0)


def first_kernel(lead_ref, inv_ref, work):
    inverse_factor(lead_ref[:, 0].reshape(NB, NB), inv_ref, work)


def second_kernel(inv0_ref, lead_ref, swapped_ref, turned_ref, right_ref, below_ref, inv_ref, work):
    core0 = lax.rem(lax.axis_index("col"), 2) == 0
    mine = lead_ref[:, 1].reshape(NB, NB)
    swapped = swapped_ref[...].reshape(NB, NB)
    inv0 = inv0_ref[...]
    turned = product3(inv0, jnp.where(core0, mine, swapped), 1, 1)
    turned_ref[...] = turned
    square = jnp.where(core0, swapped, mine) - product3(turned, turned, 0, 0)
    right = product3(inv0, lead_ref[:, 2].reshape(NB, NB), 1, 0)
    right_ref[...] = right
    below_ref[...] = lead_ref[:, 3].reshape(NB, NB) - product3(turned, right, 0, 0)
    inverse_factor(square, inv_ref, work)


def lead_kernel(first_ref, passed_ref, lead_ref):
    core0 = lax.rem(lax.axis_index("col"), 2) == 0
    lead_ref[0] = jnp.where(core0, first_ref[0], passed_ref[...])
    lead_ref[1] = first_ref[1]


def pick_kernel(lead_ref, out_ref):
    out_ref[...] = lead_ref[:, 1]


def panel_kernel(value_ref, panel_ref, mine_ref):
    panel_ref[...] = jnp.where(lax.axis_index("col") < 2, value_ref[...], 0.0)
    mine_ref[...] = value_ref[...]


def sum_kernel(*refs):
    total = refs[0][...]
    for ref in refs[1:-1]:
        total = total + ref[...]
    refs[-1][...] = total


def spread_kernel(early_ref, late_ref, base_ref, a_ref, b_ref, c_ref, order_ref, out_ref, held, sems):
    held[:2] = base_ref[...] + a_ref[...] + b_ref[...] + c_ref[...]
    held[2:] = early_ref[...] + late_ref[...]
    copies = [pltpu.make_async_copy(held, out_ref.at[t], sems.at[t]) for t in range(16)]
    for copy in copies:
        copy.start()
    for copy in copies:
        copy.wait()


def spread_pieces(early, late, lead, sent, order):
    return pl.pallas_call(
        spread_kernel,
        out_shape=jax.ShapeDtypeStruct((16, 4, 16, NB), jnp.float32),
        in_specs=[pl.BlockSpec(memory_space=pltpu.VMEM)] * 6 + [pl.BlockSpec(memory_space=pl.ANY)],
        out_specs=pl.BlockSpec(memory_space=pl.ANY),
        scratch_shapes=[pltpu.VMEM((4, 16, NB), jnp.float32), pltpu.SemaphoreType.DMA((16,))],
        compiler_params=pltpu.CompilerParams(vmem_limit_bytes=VMEM_LIMIT),
        name="spread_kernel",
    )(early, late, lead, *sent, order)


def factors_kernel(right_ref, below_ref, inv0_ref, turned_ref, inv1_ref, x0_ref, x1_ref):
    col = lax.axis_index("col")
    inv0 = inv0_ref[...]
    turned = turned_ref[...]
    inv1 = inv1_ref[...]

    @pl.when(col >= 2)
    def _():
        x1 = product3(inv1, product3(inv1, below_ref[...], 1, 0), 0, 0)
        x1_ref[...] = x1
        x0_ref[...] = product3(inv0, right_ref[...] - product3(turned, x1, 1, 0), 0, 0)

    @pl.when(col == 0)
    def _():
        x0_ref[...] = -inv0.T
        x1_ref[...] = jnp.zeros_like(inv0)

    @pl.when(col == 1)
    def _():
        x0_ref[...] = product3(inv0, product3(turned, inv1, 1, 1), 0, 0)
        x1_ref[...] = -inv1.T


def final_kernel(mine_ref, own_ref, other_ref, x0_ref, x1_ref, other0_ref, out_ref, held, sem):
    row = lax.axis_index("row")
    col = lax.axis_index("col")
    core0 = lax.rem(col, 2) == 0
    x_own = jnp.where(core0, x0_ref[...], x1_ref[...])
    x_other = jnp.where(core0, x1_ref[...], x0_ref[...])

    @pl.when(col >= 2)
    def _():
        for block in range(2):
            place = pl.ds(block * NB, NB)
            taken = product3(own_ref[place, :], x_own, 1, 0) + product3(other_ref[place, :], x_other, 1, 0)
            out_ref[place, :] = jnp.where(row + 16 * block >= 2, mine_ref[place, :] - taken, 0.0)

    @pl.when(col < 2)
    def _():
        copy = pltpu.make_async_copy(other0_ref, held, sem)
        copy.start()
        first = product3(own_ref[...], x_own, 1, 0)
        lower = lax.broadcasted_iota(jnp.int32, (NB, NB), 0) >= lax.broadcasted_iota(jnp.int32, (NB, NB), 1)
        copy.wait()
        taken = first + product3(held[...], x_other, 1, 0)
        for block in range(2):
            place = slice(block * NB, block * NB + NB)
            label = row + 16 * block
            out_ref[place, :] = jnp.where((label > col) | ((label == col) & lower), -taken[place, :], 0.0)


def call(body, out, *operands, far=(), order=(), work=False, flops=0):
    kept = len(operands)
    read = kept + len(far)
    blocks = [pltpu.VMEM] * kept + [pl.ANY] * (len(far) + len(order))
    scratch = [pltpu.VMEM((NB, NB), jnp.float32)] if work else []
    for array in far:
        scratch += [pltpu.VMEM(array.shape, array.dtype), pltpu.SemaphoreType.DMA]

    def whole(*refs):
        body(*refs[:read], *refs[read + len(order) :])

    outs = jax.tree.map(lambda shape: jax.ShapeDtypeStruct(shape, jnp.float32), out, is_leaf=lambda v: type(v[0]) is int)
    return pl.pallas_call(
        whole,
        out_shape=outs,
        in_specs=[pl.BlockSpec(memory_space=space) for space in blocks],
        scratch_shapes=scratch,
        compiler_params=pltpu.CompilerParams(vmem_limit_bytes=VMEM_LIMIT),
        cost_estimate=pl.CostEstimate(flops=flops, bytes_accessed=0, transcendentals=0) if flops else None,
        name=body.__name__,
    )(*operands, *far, *order)


def both_cores(pairs, mirror):
    out = []
    for s, t in pairs:
        out.append((2 * s, 2 * t))
        if mirror:
            s, t = (CHIPS_Z - s) % CHIPS_Z, (CHIPS_Z - t) % CHIPS_Z
        out.append((2 * s + 1, 2 * t + 1))
    return out


def swap_cores(value, chips):
    return lax.ppermute(value, "col", [(2 * z + c, 2 * z + 1 - c) for z in chips for c in (0, 1)])


def scatter_rows(top):
    return lax.all_to_all(top.reshape(16, 16, NB), "row", 0, 0)[:2]


def no_rows(top):
    return jnp.zeros((2, 16, NB), top.dtype)


def along_z(value, pairs, mirror=False):
    return lax.ppermute(value, "col", both_cores(pairs, mirror))


def local(kernel):
    square = (NB, NB)
    top = kernel[:NB]
    ten_us = 10_000_000_000

    height = lax.axis_index("col") // 2
    bottom = height == 0
    first = lax.cond(bottom, scatter_rows, no_rows, top)
    lead = call(lead_kernel, (2, 16, NB), first, lax.ppermute(first[0], "col", [(0, 1)]))
    sent = [along_z(lead, p) for p in PIECE_TREE[0]]
    waits = (height == 7) | (height == 9)
    early = lax.cond(bottom | waits, lambda t, l: l, lambda t, l: scatter_rows(t), top, lead)
    lead = call(sum_kernel, (2, 16, NB), lead, *sent, order=(early,))

    panel, mine = call(panel_kernel, (kernel.shape, kernel.shape), kernel, order=(lead,))
    other0 = swap_cores(mine, [0])
    panel = call(sum_kernel, kernel.shape, panel, along_z(panel, PANEL_TREE[0], True))
    late = lax.cond(waits, lambda t, l: scatter_rows(t), lambda t, l: no_rows(t), top, lead)
    sent = [along_z(lead, p) for p in PIECE_TREE[1]]
    spread = spread_pieces(early, late, lead, sent, panel)
    lead = lax.all_to_all(spread, "row", 0, 0)
    panel = call(sum_kernel, kernel.shape, panel, along_z(panel, PANEL_TREE[1], True), order=(spread,))
    swapped = swap_cores(call(pick_kernel, (16, 16, NB), lead, order=(panel,)), range(CHIPS_Z))
    inv0 = call(first_kernel, square, lead, order=(panel, other0), work=True, flops=ten_us)
    panel = call(sum_kernel, kernel.shape, panel, along_z(panel, PANEL_TREE[2], True), order=(inv0,))
    turned, right, below, inv1 = call(
        second_kernel, (square,) * 4, inv0, lead, swapped, order=(panel,), work=True, flops=ten_us
    )
    panel = call(sum_kernel, kernel.shape, panel, along_z(panel, PANEL_TREE[3], True), order=(inv1,))
    other = swap_cores(panel, range(1, CHIPS_Z))
    x0, x1 = call(factors_kernel, (square, square), right, below, inv0, turned, inv1, order=(panel,))
    return call(final_kernel, kernel.shape, mine, panel, other, x0, x1, far=(other0,))


def solution(mesh):
    return jax.shard_map(
        local, mesh=mesh, in_specs=(P("row", "col"),), out_specs=P("row", "col"), check_vma=False
    )
```

```python
import jax
import jax.numpy as jnp
from jax import lax
from jax.experimental import pallas as pl
from jax.experimental.pallas import tpu as pltpu
from jax.sharding import PartitionSpec as P

NB = 256
BASE = 32
LANES = 128
SUBS = 8
VMEM_LIMIT = 6 * 1024 * 1024

CHIPS_Z = 16
PANEL_TREE = (
    ((0, 7),),
    ((0, 4), (7, 11)),
    ((0, 2), (7, 6), (4, 8), (11, 13)),
    ((0, 15), (2, 1), (4, 3), (6, 5), (7, 10), (8, 9), (11, 12), (13, 14)),
)
PIECE_TREE = (
    (((0, 12),), ((0, 4),), ((0, 8),)),
    (
        tuple((s, s + 1) for s in (0, 4, 8, 12)),
        tuple((s, (s + 15) % 16) for s in (0, 4, 8, 12)),
        tuple((s, s + 2) for s in (0, 4, 8, 12)),
    ),
)


def split(a):
    high = a.astype(jnp.bfloat16)
    return high, (a - high.astype(jnp.float32)).astype(jnp.bfloat16)


def product3(a, b, a_dim, b_dim):
    dims = (((a_dim,), (b_dim,)), ((), ()))
    a_high, a_low = split(a)
    b_high, b_low = split(b)

    def dot(x, y):
        return lax.dot_general(x, y, dims, preferred_element_type=jnp.float32)

    return dot(a_high, b_high) + (dot(a_high, b_low) + dot(a_low, b_high))


def small_inverse(rows, off):
    groups = BASE // SUBS
    lane = lax.broadcasted_iota(jnp.int32, (SUBS, LANES), 1)
    sub = lax.broadcasted_iota(jnp.int32, (SUBS, LANES), 0)
    cols = [[None] * groups for _ in range(BASE)]
    for c in range(BASE):
        for q in range(c // SUBS, groups):
            piece = rows[SUBS * q : SUBS * q + SUBS, off + c : off + c + 1]
            cols[c][q] = jnp.broadcast_to(piece, (SUBS, LANES))
    inv = [jnp.where(lane == sub + (off + SUBS * q), 1.0, 0.0) for q in range(groups)]
    scale = []
    for k in range(BASE):
        qk, rk = divmod(k, SUBS)
        root = lax.rsqrt(jnp.broadcast_to(cols[k][qk][rk : rk + 1], (SUBS, LANES)))
        recip = root * root
        scaled = [None if part is None else part * recip for part in cols[k]]
        for c in range(k + 1, BASE):
            qc, rc = divmod(c, SUBS)
            factor = jnp.broadcast_to(cols[k][qc][rc : rc + 1], (SUBS, LANES))
            for q in range(qc, groups):
                cols[c][q] = cols[c][q] - scaled[q] * factor
        row = jnp.broadcast_to(inv[qk][rk : rk + 1], (SUBS, LANES)) * recip
        for q in range(qk, groups):
            update = cols[k][q] * row
            if q == qk:
                update = jnp.where(sub > rk, update, 0.0)
            inv[q] = inv[q] - update
        scale.append(root)
    out = []
    for q in range(groups):
        factor = scale[SUBS * q]
        for r in range(1, SUBS):
            factor = jnp.where(sub == r, scale[SUBS * q + r], factor)
        out.append(inv[q] * factor)
    return jnp.concatenate(out, axis=0)


def inverse_factor(square, out_ref, work):
    work[...] = square
    for low in range(0, NB, BASE):
        tile = low // LANES * LANES
        off = low - tile
        high = low + BASE
        small = small_inverse(work[low:high, tile : tile + LANES], off)
        block = small[:, off : off + BASE]
        strip = product3(block, work[low:high, :], 1, 0)
        lane = lax.broadcasted_iota(jnp.int32, (BASE, LANES), 1)
        own = jnp.where((lane >= off) & (lane < off + BASE), small, strip[:, tile : tile + LANES])
        strip = jnp.concatenate(
            [own if t == tile else strip[:, t : t + LANES] for t in range(0, NB, LANES)], axis=1
        )
        out_ref[low:high, :] = strip
        for first, last in ((high, high + BASE), (high + BASE, NB)):
            if first < last <= NB:
                left = product3(work[first:last, low:high], block, 1, 1)
                old = work[first:last, :]
                lanes = lax.broadcasted_iota(jnp.int32, old.shape, 1)
                old = jnp.where((lanes >= low) & (lanes < high), 0.0, old)
                work[first:last, :] = old - product3(left, strip, 1, 0)
    rows = lax.broadcasted_iota(jnp.int32, (NB, NB), 0)
    cols = lax.broadcasted_iota(jnp.int32, (NB, NB), 1)
    out_ref[...] = jnp.where(rows >= cols, out_ref[...], 0.0)


def first_kernel(lead_ref, inv_ref, work):
    inverse_factor(lead_ref[:, 0].reshape(NB, NB), inv_ref, work)


def second_kernel(inv0_ref, lead_ref, swapped_ref, turned_ref, right_ref, below_ref, inv_ref, work):
    core0 = lax.rem(lax.axis_index("col"), 2) == 0
    mine = lead_ref[:, 1].reshape(NB, NB)
    swapped = swapped_ref[...].reshape(NB, NB)
    inv0 = inv0_ref[...]
    turned = product3(inv0, jnp.where(core0, mine, swapped), 1, 1)
    turned_ref[...] = turned
    square = jnp.where(core0, swapped, mine) - product3(turned, turned, 0, 0)
    right = product3(inv0, lead_ref[:, 2].reshape(NB, NB), 1, 0)
    right_ref[...] = right
    below_ref[...] = lead_ref[:, 3].reshape(NB, NB) - product3(turned, right, 0, 0)
    inverse_factor(square, inv_ref, work)


def lead_kernel(first_ref, passed_ref, lead_ref):
    core0 = lax.rem(lax.axis_index("col"), 2) == 0
    lead_ref[0] = jnp.where(core0, first_ref[0], passed_ref[...])
    lead_ref[1] = first_ref[1]


def pick_kernel(lead_ref, out_ref):
    out_ref[...] = lead_ref[:, 1]


def panel_kernel(value_ref, panel_ref, mine_ref):
    panel_ref[...] = jnp.where(lax.axis_index("col") < 2, value_ref[...], 0.0)
    mine_ref[...] = value_ref[...]


def sum_kernel(*refs):
    total = refs[0][...]
    for ref in refs[1:-1]:
        total = total + ref[...]
    refs[-1][...] = total


def spread_kernel(early_ref, late_ref, base_ref, a_ref, b_ref, c_ref, order_ref, out_ref, held, sems):
    held[:2] = base_ref[...] + a_ref[...] + b_ref[...] + c_ref[...]
    held[2:] = early_ref[...] + late_ref[...]
    copies = [pltpu.make_async_copy(held, out_ref.at[t], sems.at[t]) for t in range(16)]
    for copy in copies:
        copy.start()
    for copy in copies:
        copy.wait()


def spread_pieces(early, late, lead, sent, order):
    return pl.pallas_call(
        spread_kernel,
        out_shape=jax.ShapeDtypeStruct((16, 4, 16, NB), jnp.float32),
        in_specs=[pl.BlockSpec(memory_space=pltpu.VMEM)] * 6 + [pl.BlockSpec(memory_space=pl.ANY)],
        out_specs=pl.BlockSpec(memory_space=pl.ANY),
        scratch_shapes=[pltpu.VMEM((4, 16, NB), jnp.float32), pltpu.SemaphoreType.DMA((16,))],
        compiler_params=pltpu.CompilerParams(vmem_limit_bytes=VMEM_LIMIT),
        name="spread_kernel",
    )(early, late, lead, *sent, order)


def factors_kernel(right_ref, below_ref, inv0_ref, turned_ref, inv1_ref, x0_ref, x1_ref):
    col = lax.axis_index("col")
    inv0 = inv0_ref[...]
    turned = turned_ref[...]
    inv1 = inv1_ref[...]

    @pl.when(col >= 2)
    def _():
        x1 = product3(inv1, product3(inv1, below_ref[...], 1, 0), 0, 0)
        x1_ref[...] = x1
        x0_ref[...] = product3(inv0, right_ref[...] - product3(turned, x1, 1, 0), 0, 0)

    @pl.when(col == 0)
    def _():
        x0_ref[...] = -inv0.T
        x1_ref[...] = jnp.zeros_like(inv0)

    @pl.when(col == 1)
    def _():
        x0_ref[...] = product3(inv0, product3(turned, inv1, 1, 1), 0, 0)
        x1_ref[...] = -inv1.T


def final_kernel(mine_ref, own_ref, other_ref, x0_ref, x1_ref, other0_ref, out_ref, held, sem):
    row = lax.axis_index("row")
    col = lax.axis_index("col")
    core0 = lax.rem(col, 2) == 0
    x_own = jnp.where(core0, x0_ref[...], x1_ref[...])
    x_other = jnp.where(core0, x1_ref[...], x0_ref[...])

    @pl.when(col >= 2)
    def _():
        for block in range(2):
            place = pl.ds(block * NB, NB)
            taken = product3(own_ref[place, :], x_own, 1, 0) + product3(other_ref[place, :], x_other, 1, 0)
            out_ref[place, :] = jnp.where(row + 16 * block >= 2, mine_ref[place, :] - taken, 0.0)

    @pl.when(col < 2)
    def _():
        copy = pltpu.make_async_copy(other0_ref, held, sem)
        copy.start()
        first = product3(own_ref[...], x_own, 1, 0)
        lower = lax.broadcasted_iota(jnp.int32, (NB, NB), 0) >= lax.broadcasted_iota(jnp.int32, (NB, NB), 1)
        copy.wait()
        taken = first + product3(held[...], x_other, 1, 0)
        for block in range(2):
            place = slice(block * NB, block * NB + NB)
            label = row + 16 * block
            out_ref[place, :] = jnp.where((label > col) | ((label == col) & lower), -taken[place, :], 0.0)


def call(body, out, *operands, far=(), order=(), work=False, flops=0):
    kept = len(operands)
    read = kept + len(far)
    blocks = [pltpu.VMEM] * kept + [pl.ANY] * (len(far) + len(order))
    scratch = [pltpu.VMEM((NB, NB), jnp.float32)] if work else []
    for array in far:
        scratch += [pltpu.VMEM(array.shape, array.dtype), pltpu.SemaphoreType.DMA]

    def whole(*refs):
        body(*refs[:read], *refs[read + len(order) :])

    outs = jax.tree.map(lambda shape: jax.ShapeDtypeStruct(shape, jnp.float32), out, is_leaf=lambda v: type(v[0]) is int)
    return pl.pallas_call(
        whole,
        out_shape=outs,
        in_specs=[pl.BlockSpec(memory_space=space) for space in blocks],
        scratch_shapes=scratch,
        compiler_params=pltpu.CompilerParams(vmem_limit_bytes=VMEM_LIMIT),
        cost_estimate=pl.CostEstimate(flops=flops, bytes_accessed=0, transcendentals=0) if flops else None,
        name=body.__name__,
    )(*operands, *far, *order)


def both_cores(pairs, mirror):
    out = []
    for s, t in pairs:
        out.append((2 * s, 2 * t))
        if mirror:
            s, t = (CHIPS_Z - s) % CHIPS_Z, (CHIPS_Z - t) % CHIPS_Z
        out.append((2 * s + 1, 2 * t + 1))
    return out


def swap_cores(value, chips):
    return lax.ppermute(value, "col", [(2 * z + c, 2 * z + 1 - c) for z in chips for c in (0, 1)])


def scatter_rows(top):
    return lax.all_to_all(top.reshape(16, 16, NB), "row", 0, 0)[:2]


def no_rows(top):
    return jnp.zeros((2, 16, NB), top.dtype)


def along_z(value, pairs, mirror=False):
    return lax.ppermute(value, "col", both_cores(pairs, mirror))


def local(kernel):
    square = (NB, NB)
    top = kernel[:NB]
    ten_us = 10_000_000_000

    height = lax.axis_index("col") // 2
    bottom = height == 0
    first = lax.cond(bottom, scatter_rows, no_rows, top)
    lead = call(lead_kernel, (2, 16, NB), first, lax.ppermute(first[0], "col", [(0, 1)]))
    sent = [along_z(lead, p) for p in PIECE_TREE[0]]
    waits = (height == 7) | (height == 9)
    early = lax.cond(bottom | waits, lambda t, l: l, lambda t, l: scatter_rows(t), top, lead)
    lead = call(sum_kernel, (2, 16, NB), lead, *sent, order=(early,))

    panel, mine = call(panel_kernel, (kernel.shape, kernel.shape), kernel, order=(lead,))
    other0 = swap_cores(mine, [0])
    panel = call(sum_kernel, kernel.shape, panel, along_z(panel, PANEL_TREE[0], True))
    late = lax.cond(waits, lambda t, l: scatter_rows(t), lambda t, l: no_rows(t), top, lead)
    sent = [along_z(lead, p) for p in PIECE_TREE[1]]
    spread = spread_pieces(early, late, lead, sent, panel)
    lead = lax.all_to_all(spread, "row", 0, 0)
    panel = call(sum_kernel, kernel.shape, panel, along_z(panel, PANEL_TREE[1], True), order=(spread,))
    swapped = swap_cores(call(pick_kernel, (16, 16, NB), lead, order=(panel,)), range(CHIPS_Z))
    inv0 = call(first_kernel, square, lead, order=(panel, other0), work=True, flops=ten_us)
    panel = call(sum_kernel, kernel.shape, panel, along_z(panel, PANEL_TREE[2], True), order=(inv0,))
    turned, right, below, inv1 = call(
        second_kernel, (square,) * 4, inv0, lead, swapped, order=(panel,), work=True, flops=ten_us
    )
    panel = call(sum_kernel, kernel.shape, panel, along_z(panel, PANEL_TREE[3], True), order=(inv1,))
    other = swap_cores(panel, range(1, CHIPS_Z))
    x0, x1 = call(factors_kernel, (square, square), right, below, inv0, turned, inv1, order=(panel,))
    return call(final_kernel, kernel.shape, mine, panel, other, x0, x1, far=(other0,))


def solution(mesh):
    return jax.shard_map(
        local, mesh=mesh, in_specs=(P("row", "col"),), out_specs=P("row", "col"), check_vma=False
    )
```
